512 devices in a mesh: grp: 4 (over y_hi), seq: 16 (over z, core), voc: 8 (over x, y_lo).
Axes of the slice: x: 4, y: 8 (y_hi: 4, y_lo: 2; y = y_hi * 2 + y_lo), z: 8, core: 2. Of those that a mesh axis runs over, the one named last changes fastest.
Arguments:
- residual: bfloat16 [1536, 12288], P(('grp', 'voc'), 'seq'), may hold values from -36 to 36
- norm_gain: float32 [12288], P('seq'), may hold values from 0.5 to 1.5
- head_weight: bfloat16 [16384, 12288], P(('grp', 'voc'), 'seq'), may hold values from -1 to 1
- actions: int32 [1536], replicated, may hold values from 0 to 16383
- behavior_logp: float32 [1536], replicated, may hold values from -30 to -14
- advantages: float32 [1536], replicated, may hold values from -4 to 4
- decision_mask: int32 [1536], replicated, may hold values 0 or 1
- clip_tenths: int32 [1536], replicated, may hold values from 5 to 20
Outputs:
- loss: float32 [], replicated
- head_grad: bfloat16 [16384, 12288], P(('grp', 'voc'), 'seq')
- hidden_grad: float32 [1536, 12288], P(('grp', 'voc'), 'seq')
The draws below stay inside these ranges and needn't reach their ends.
All inputs are finite; a program needn't handle non-finite values.
Results may differ from the reference program's by a relative error of at most 0.01875.
Values may be sent and summed in bfloat16 or wider, within the bound.
A program may use at most 64 MiB of HBM per device.

```python
import jax
import jax.numpy as jnp
from jax import lax

D = 12288
VOCAB = 16384
TOKENS = 1536
VBLK = 512


def residual_values(key, lowest):
    subkeys = jax.random.split(key, 3)
    normals = jax.random.truncated_normal(subkeys[0], -4.0, 4.0, (TOKENS, D), jnp.float32)
    row_scale = jnp.exp(jax.random.uniform(subkeys[1], (TOKENS, 1), jnp.float32, jnp.log(lowest), jnp.log(3.0)))
    col_scale = jnp.exp(jax.random.uniform(subkeys[2], (1, D), jnp.float32, jnp.log(0.3), jnp.log(3.0)))
    return normals * row_scale * col_scale


def draw_residual(key, part):
    values = residual_values(key, 0.3)
    return values.astype(jnp.bfloat16)


def draw_head_weight(key, part):
    key = jax.random.fold_in(key, 11)
    subkeys = jax.random.split(key, 2)
    normals = jax.random.truncated_normal(subkeys[0], -4.0, 4.0, (VOCAB, D), jnp.float32)
    row_scale = jnp.exp(jax.random.uniform(subkeys[1], (VOCAB, 1), jnp.float32, 0.0, jnp.log(6.0)))
    matrix = normals * row_scale / jnp.sqrt(jnp.float32(D))
    return matrix.astype(jnp.bfloat16)


def place_ends(entries, key, least, high):
    index_at = [jax.random.randint(jax.random.fold_in(key, axis), (), 0, length) for axis, length in enumerate(entries.shape)]
    widest = entries.shape.index(max(entries.shape))
    beside = index_at[:widest] + [(index_at[widest] + 1) % entries.shape[widest]] + index_at[widest + 1:]
    return entries.at[tuple(index_at)].set(least).at[tuple(beside)].set(high)


def gaussian(rng, extent, deviation, most, held_as=jnp.bfloat16):
    values = deviation * jax.random.normal(rng, extent, jnp.float32)
    return jnp.clip(values, min=-most, max=most).astype(held_as)


def setup_inputs(seed: int = 0) -> dict:
    streams_of = jax.random.split(jax.random.key(seed), 9)
    residual = draw_residual(jax.random.fold_in(streams_of[8], 71), 0)
    norm_gain = jnp.clip(1.0 + 0.1 * jax.random.normal(streams_of[1], (D,), jnp.float32), 0.5, 1.5)
    head_weight = draw_head_weight(jax.random.fold_in(streams_of[8], 71), 0)
    actions = place_ends(jax.random.randint(streams_of[3], (TOKENS,), 0, VOCAB), jax.random.fold_in(streams_of[3], 1), 0, VOCAB - 1).astype(jnp.int32)
    behavior_logp = jnp.clip(jax.random.uniform(streams_of[4], (TOKENS,), jnp.float32, -30.0, -14.0), -30.0, -14.0)
    advantages = gaussian(streams_of[5], (TOKENS,), 1.0, 4.0, jnp.float32)
    decision_mask = place_ends((jax.random.randint(streams_of[6], (TOKENS,), 0, 4) < 3).astype(jnp.int32), jax.random.fold_in(streams_of[6], 1), 0, 1)
    clip_tenths = place_ends(jax.random.randint(streams_of[7], (TOKENS,), 5, 21), jax.random.fold_in(streams_of[7], 1), 5, 20).astype(jnp.int32)
    return {"residual": residual, "norm_gain": norm_gain, "head_weight": head_weight, "actions": actions, "behavior_logp": behavior_logp, "advantages": advantages, "decision_mask": decision_mask, "clip_tenths": clip_tenths}


EPSILON = 1e-05
GRAD_SCALE = 8.0

def rounded(values):
    narrow = lax.optimization_barrier(values.astype(jnp.bfloat16))
    return narrow.astype(jnp.float32)

def reference(residual, norm_gain, head_weight, actions, behavior_logp, advantages, decision_mask, clip_tenths):
    wide_rows = residual.astype(jnp.float32)
    inv_rms = lax.rsqrt(lax.optimization_barrier(jnp.mean(wide_rows * wide_rows, axis=1)) + EPSILON)
    unit_rows = wide_rows * inv_rms[:, None]
    hidden = (unit_rows * norm_gain[None, :]).astype(jnp.bfloat16)
    hidden_wide = hidden.astype(jnp.float32)
    weight_wide = head_weight.astype(jnp.float32)
    logits = jnp.einsum('td,vd->tv', hidden_wide, weight_wide, precision=lax.Precision.HIGHEST)
    row_top = lax.optimization_barrier(jnp.max(logits, axis=1))
    exp_total = lax.optimization_barrier(jnp.sum(jnp.exp(logits - row_top[:, None]), axis=1))
    log_norm = row_top + jnp.log(exp_total)
    columns = jnp.arange(VOCAB, dtype=jnp.int32)
    is_taken = columns[None, :] == actions.astype(jnp.int32)[:, None]
    picked = lax.optimization_barrier(jnp.sum(jnp.where(is_taken, logits, 0.0), axis=1))
    log_prob = picked - log_norm
    trunc_level = clip_tenths.astype(jnp.float32) / 10.0
    ratio_weight = jnp.minimum(jnp.exp(log_prob - behavior_logp), trunc_level)
    decisions = decision_mask.astype(jnp.float32)
    scaled = decisions * ratio_weight * advantages
    loss = -jnp.sum(scaled * log_prob) / TOKENS
    softmax = jnp.exp(logits - log_norm[:, None])
    dlogits = ((GRAD_SCALE * scaled)[:, None] * (softmax - is_taken.astype(jnp.float32))).astype(jnp.bfloat16)
    dlogits_wide = dlogits.astype(jnp.float32)
    head_grad = jnp.einsum('tv,td->vd', dlogits_wide, hidden_wide, precision=lax.Precision.HIGHEST).astype(jnp.bfloat16)

    def add_vocab_block(block_index, running):
        first_row = (block_index * VBLK).astype(jnp.int32)
        left_part = lax.dynamic_slice_in_dim(dlogits_wide, first_row, VBLK, 1)
        right_part = lax.dynamic_slice_in_dim(weight_wide, first_row, VBLK, 0)
        product = jnp.dot(left_part, right_part, precision=lax.Precision.HIGHEST)
        return running + rounded(product)
    hidden_grad = lax.fori_loop(0, VOCAB // VBLK, add_vocab_block, jnp.zeros((TOKENS, D), jnp.float32))
    return (loss, head_grad, hidden_grad)
```

```python
import functools

import jax
import jax.numpy as jnp
from jax import lax
from jax.experimental import pallas as pl
from jax.experimental.pallas import tpu as pltpu
from jax.sharding import PartitionSpec as P

EPSILON = 1e-05
GRAD_SCALE = 8.0
NX = 4
ROWS = 16
SKEW = 4
LANES = 128
F32 = jnp.float32
BF16 = jnp.bfloat16


def as_rows(columns):
    n = columns.shape[0]
    if n < LANES:
        columns = jnp.concatenate([columns, jnp.zeros((LANES - n, LANES), F32)], axis=0)
    return columns.T[:8]


def as_columns(rows, n):
    full = jnp.concatenate([rows, jnp.zeros((LANES - 8, LANES), F32)], axis=0)
    return full.T[:n]


def stack_rows(*rows):
    index = lax.broadcasted_iota(jnp.int32, (8, LANES), 0)
    out = jnp.zeros((8, LANES), F32)
    for i, row in enumerate(rows):
        out = jnp.where(index == i, jnp.broadcast_to(row, (8, LANES)), out)
    return out


def combine(tiles):
    top = tiles[0][0:1]
    for t in tiles[1:]:
        top = jnp.maximum(top, t[0:1])
    total = jnp.zeros_like(top)
    picked = jnp.zeros_like(top)
    for t in tiles:
        total = total + t[1:2] * jnp.exp(t[0:1] - top)
        picked = picked + t[2:3]
    return top, total, picked


def kernel(
    ny, nz, nc, res_ref, gain_ref, w_ref, tok_ref,
    loss_ref, head_ref, hid_ref,
    sqc, sqz, H, L, xs, xr, cs, cr, lg, dyb, dxb, DL, PB, g1, g2, gs, qf, qs, qr, acc, lossc, lossz,
    ssem, rsem,
):
    grp, seq, voc = lax.axis_index("grp"), lax.axis_index("seq"), lax.axis_index("voc")
    x, y = lax.div(voc, 2), grp * 2 + lax.rem(voc, 2)
    z, c = lax.div(seq, 2), lax.rem(seq, 2)
    oc = 1 - c
    vl, dl_width = w_ref.shape
    d_total = dl_width * nz * 2
    tp = ROWS * NX * ny // (nz * 2)
    half = ny // 2
    left, right, opp = lax.rem(x + 3, NX), lax.rem(x + 1, NX), lax.rem(x + 2, NX)

    def dev(x=x, y=y, z=z, c=c):
        return {"grp": lax.div(y, 2), "seq": z * 2 + c, "voc": x * 2 + lax.rem(y, 2)}

    ys = [lax.rem(y + d, ny) for d in range(1, ny)]
    zs = [lax.rem(z + d, nz) for d in range(1, nz)]
    xs_ = [lax.rem(x + d, NX) for d in range(1, NX)]

    started = []

    def send(src, dst, target):
        i = len(started)
        cp = pltpu.make_async_remote_copy(
            src_ref=src, dst_ref=dst, send_sem=ssem.at[i], recv_sem=rsem.at[i],
            device_id=target, device_id_type=pl.DeviceIdType.MESH,
        )
        cp.start()
        started.append(cp)
        return cp

    def arrive(copies):
        for cp in copies:
            cp.wait_recv()

    barrier = pltpu.get_barrier_semaphore()
    partners = (
        [dev(y=t) for t in ys] + [dev(z=t) for t in zs] + [dev(x=t) for t in xs_] + [dev(c=oc)]
    )
    for p in partners:
        pl.semaphore_signal(barrier, inc=1, device_id=p, device_id_type=pl.DeviceIdType.MESH)

    own = res_ref[...].astype(F32)
    n_own = own.shape[0]
    sq = own * own
    part = sq[:, :LANES]
    for j in range(LANES, dl_width, LANES):
        part = part + sq[:, j : j + LANES]
    part = jnp.concatenate([part, jnp.zeros((LANES - n_own, LANES), F32)], axis=0)
    sqc[c] = jnp.broadcast_to(jnp.sum(part.T, axis=0, keepdims=True), (8, LANES))
    pl.semaphore_wait(barrier, len(partners))
    arrive([send(sqc.at[c], sqc.at[c], dev(c=oc))])
    sqz[z] = sqc[0] + sqc[1]
    arrive([send(sqz.at[z], sqz.at[z], dev(z=t)) for t in zs])
    squares = sqz[0]
    for i in range(1, nz):
        squares = squares + sqz[i]
    inv = lax.rsqrt(squares / d_total + EPSILON)
    inv = jnp.broadcast_to(inv[0:1], (LANES, LANES)).T[:n_own]
    inv = jnp.concatenate([inv] * (dl_width // LANES), axis=1)
    hidden = (own * inv * gain_ref[...]).astype(BF16)
    gathers = []
    for k in range(nc):
        H[k, x, y] = hidden[k * ROWS : (k + 1) * ROWS]
        gathers.append([send(H.at[k, x, y], H.at[k, x, y], dev(y=t)) for t in ys])

    lane = lax.broadcasted_iota(jnp.int32, (1, LANES), 1)
    losses = []
    zt = half

    def chunk(k):
        arrive(gathers[k])
        a = [send(H.at[k, x], H.at[k, x], dev(x=t)) for t in (right, left)]
        yield
        arrive(a)
        a = [
            send(H.at[k, left, pl.ds(0, half)], H.at[k, left, pl.ds(0, half)], dev(x=right)),
            send(H.at[k, right, pl.ds(half, half)], H.at[k, right, pl.ds(half, half)], dev(x=left)),
        ]
        yield
        arrive(a)

        @pl.loop(0, NX // 2)
        def _(i):
            h = H[k, pl.ds(2 * i, 2)].reshape(2 * ny * ROWS, dl_width)
            t = lax.dot_general(h, w_ref[...], (((1,), (1,)), ((), ())), preferred_element_type=F32)
            L[k, pl.ds(zt * i, zt)] = t.reshape(zt, 2, tp, vl)

        for i in range(nz):
            xs[k, i] = L[k, i, oc].astype(BF16)
        a = [send(xs.at[k], xr.at[k], dev(c=oc))]
        yield
        arrive(a)
        for i in range(nz):
            cs[k, i] = (L[k, i, c] + xr[k, i].astype(F32)).astype(BF16)
        a = [send(cs.at[k, t], cr.at[k, z], dev(z=t)) for t in zs]
        yield
        arrive(a)
        logits = L[k, z, c] + xr[k, z].astype(F32)
        for t in zs:
            logits = logits + cr[k, t].astype(F32)
        lg[k] = logits

        tok = tok_ref[k]
        first_row = ((grp * NX * 2 + voc) * vl).astype(F32)
        column = lax.broadcasted_iota(jnp.int32, (tp, vl), 1).astype(F32)
        taken = column == as_columns(tok, tp)[:, 0:1] - first_row
        top = jnp.max(logits, axis=1, keepdims=True)
        total = jnp.sum(jnp.exp(logits - top), axis=1, keepdims=True)
        picked = jnp.sum(jnp.where(taken, logits, 0.0), axis=1, keepdims=True)
        at = lax.broadcasted_iota(jnp.int32, (tp, LANES), 1)
        dyb[k, y] = as_rows(
            jnp.where(at == 0, top, jnp.where(at == 1, total, jnp.where(at == 2, picked, 0.0)))
        )
        a = [send(dyb.at[k, y], dyb.at[k, y], dev(y=t)) for t in ys]
        yield
        arrive(a)
        dxb[k, x] = stack_rows(*combine([dyb[k, i] for i in range(ny)]))
        a = [send(dxb.at[k, x], dxb.at[k, x], dev(x=t)) for t in xs_]
        yield
        arrive(a)
        top, total, picked = combine([dxb[k, i] for i in range(NX)])
        is_own = lane < tp
        log_norm = top + jnp.log(jnp.where(is_own, total, 1.0))
        log_prob = picked - log_norm
        ratio = jnp.minimum(jnp.exp(log_prob - tok[1:2]), tok[4:5])
        scaled = tok[3:4] * ratio * tok[2:3]
        losses.append(jnp.sum(jnp.where(is_own, scaled * log_prob, 0.0), axis=1, keepdims=True))
        cols = as_columns(stack_rows(log_norm, GRAD_SCALE * scaled, tok[0:1]), tp)
        taken = column == cols[:, 2:3] - first_row
        softmax = jnp.exp(lg[k] - cols[:, 0:1])
        DL[k, z, c] = (cols[:, 1:2] * (softmax - taken.astype(F32))).astype(BF16)
        a = [send(DL.at[k, z, c], DL.at[k, z, c], dev(z=t)) for t in zs]
        last = k == nc - 1
        if last:
            lossc[c] = jnp.broadcast_to(sum(losses[1:], losses[0]), (8, LANES))
            b = [send(lossc.at[c], lossc.at[c], dev(c=oc))]
        yield
        arrive(a)
        a = [send(DL.at[k, :, c], DL.at[k, :, c], dev(c=oc))]
        if last:
            arrive(b)
            lossz[z] = lossc[0] + lossc[1]
            b = [send(lossz.at[z], lossz.at[z], dev(z=t)) for t in zs]
        yield
        arrive(a)

        @pl.loop(0, NX // 2)
        def _(i):
            d = DL[k, pl.ds(zt * i, zt)].reshape(2 * ny * ROWS, vl)
            t = jnp.dot(d, w_ref[...], preferred_element_type=F32).astype(BF16)
            PB[k, pl.ds(2 * i, 2)] = t.reshape(2, ny, ROWS, dl_width)

        low, high = pl.ds(0, half), pl.ds(half, half)
        a = [
            send(PB.at[k, opp, low], g1.at[k, 0], dev(x=left)),
            send(PB.at[k, opp, high], g1.at[k, 1], dev(x=right)),
        ]
        b2 = [
            send(PB.at[k, left, high], g2.at[k, 0, high], dev(x=left)),
            send(PB.at[k, right, low], g2.at[k, 1, low], dev(x=right)),
        ]
        h_all = H[k].reshape(NX * ny * ROWS, dl_width)
        d_all = DL[k].reshape(NX * ny * ROWS, vl)
        t = lax.dot_general(d_all, h_all, (((0,), (0,)), ((), ())), preferred_element_type=F32)
        if nc == 1:
            head_ref[...] = t.astype(BF16)
        elif k == 0:
            acc[...] = t
        elif last:
            head_ref[...] = (acc[...] + t).astype(BF16)
        else:
            acc[...] += t
        yield
        arrive(a)
        gs[k, 0] = (PB[k, left, low].astype(F32) + g1[k, 0].astype(F32)).astype(BF16)
        b2.append(send(gs.at[k, 0], g2.at[k, 0, low], dev(x=left)))
        gs[k, 1] = (PB[k, right, high].astype(F32) + g1[k, 1].astype(F32)).astype(BF16)
        b2.append(send(gs.at[k, 1], g2.at[k, 1, high], dev(x=right)))
        yield
        arrive(b2)
        for i in range(ny):
            q = PB[k, x, i].astype(F32) + g2[k, 0, i].astype(F32) + g2[k, 1, i].astype(F32)
            qf[k, i] = q
            qs[k, i] = q.astype(BF16)
        a = [send(qs.at[k, t], qr.at[k, y], dev(y=t)) for t in ys]
        yield
        arrive(a)
        q = qf[k, y]
        for t in ys:
            q = q + qr[k, t].astype(F32)
        hid_ref[k * ROWS : (k + 1) * ROWS, :] = q
        if last:
            arrive(b)
            loss = lossz[0]
            for i in range(1, nz):
                loss = loss + lossz[i]
            loss_ref[...] = loss * (-1.0 / (n_own * NX * ny))

    runs = [chunk(k) for k in range(nc)]
    slot = 0
    while any(r is not None for r in runs):
        for k in range(nc):
            if slot >= k * SKEW and runs[k] is not None:
                try:
                    next(runs[k])
                except StopIteration:
                    runs[k] = None
        slot += 1
    for cp in started:
        cp.wait_send()


def per_device(mesh_sizes, residual, norm_gain, head_weight, actions, behavior_logp, advantages, decision_mask, clip_tenths):
    n_grp, n_seq, n_voc = mesh_sizes
    ny, nz = n_grp * 2, n_seq // 2
    n_own, dw = residual.shape
    vl = head_weight.shape[0]
    nc = n_own // ROWS
    tp = ROWS * NX * ny // n_seq

    seq = lax.axis_index("seq")
    pairs = [actions.astype(F32), behavior_logp, advantages, decision_mask.astype(F32), clip_tenths.astype(F32) / 10.0]
    tok = jnp.stack(pairs).reshape(5, n_seq, 2, nc, ROWS)
    where = lax.rem(2 * seq, ny) // 2 * NX + lax.div(2 * seq, ny)
    tok = lax.dynamic_index_in_dim(tok, where, 1, keepdims=False)
    tok = tok.transpose(2, 0, 1, 3).reshape(nc, 5, tp)
    tok = jnp.pad(tok, ((0, 0), (0, 3), (0, LANES - tp)))

    n_sends = (1 + nz - 1) + nc * (3 * (ny - 1) + 2 * (nz - 1) + 2 + 2 + 1 + 3 + 1 + 6) + 1 + nz - 1
    vm = pl.BlockSpec(memory_space=pltpu.VMEM)
    tile = (8, LANES)
    loss, head_grad, hidden_grad = pl.pallas_call(
        functools.partial(kernel, ny, nz, nc),
        out_shape=(
            jax.ShapeDtypeStruct(tile, F32),
            jax.ShapeDtypeStruct((vl, dw), BF16),
            jax.ShapeDtypeStruct((n_own, dw), F32),
        ),
        in_specs=[vm] * 4,
        out_specs=(vm, vm, vm),
        scratch_shapes=[
            pltpu.VMEM((2,) + tile, F32),
            pltpu.VMEM((nz,) + tile, F32),
            pltpu.VMEM((nc, NX, ny, ROWS, dw), BF16),
            pltpu.VMEM((nc, nz, 2, tp, vl), F32),
            pltpu.VMEM((nc, nz, tp, vl), BF16),
            pltpu.VMEM((nc, nz, tp, vl), BF16),
            pltpu.VMEM((nc, nz, tp, vl), BF16),
            pltpu.VMEM((nc, nz, tp, vl), BF16),
            pltpu.VMEM((nc, tp, vl), F32),
            pltpu.VMEM((nc, ny) + tile, F32),
            pltpu.VMEM((nc, NX) + tile, F32),
            pltpu.VMEM((nc, nz, 2, tp, vl), BF16),
            pltpu.VMEM((nc, NX, ny, ROWS, dw), BF16),
            pltpu.VMEM((nc, 2, ny // 2, ROWS, dw), BF16),
            pltpu.VMEM((nc, 2, ny, ROWS, dw), BF16),
            pltpu.VMEM((nc, 2, ny // 2, ROWS, dw), BF16),
            pltpu.VMEM((nc, ny, ROWS, dw), F32),
            pltpu.VMEM((nc, ny, ROWS, dw), BF16),
            pltpu.VMEM((nc, ny, ROWS, dw), BF16),
            pltpu.VMEM((vl, dw), F32),
            pltpu.VMEM((2,) + tile, F32),
            pltpu.VMEM((nz,) + tile, F32),
            pltpu.SemaphoreType.DMA((n_sends,)),
            pltpu.SemaphoreType.DMA((n_sends,)),
        ],
        compiler_params=pltpu.CompilerParams(
            collective_id=0, has_side_effects=True, vmem_limit_bytes=56 * 2**20
        ),
    )(residual, norm_gain.reshape(1, dw), head_weight, tok)
    return loss[0, 0], head_grad, hidden_grad


def solution(mesh):
    sizes = (mesh.shape["grp"], mesh.shape["seq"], mesh.shape["voc"])
    split = P(("grp", "voc"), "seq")
    return jax.shard_map(
        functools.partial(per_device, sizes),
        mesh=mesh,
        in_specs=(split, P("seq"), split, P(), P(), P(), P(), P()),
        out_specs=(P(), split, split),
        check_vma=False,
    )
```

```python
import functools

import jax
import jax.numpy as jnp
from jax import lax
from jax.experimental import pallas as pl
from jax.experimental.pallas import tpu as pltpu
from jax.sharding import PartitionSpec as P

EPSILON = 1e-05
GRAD_SCALE = 8.0
NX = 4
ROWS = 16
STAGGER = 6.0
READY = (7.0, 13.5, 16.2, 17.0, 18.5, 19.5, 24.0, 25.0, 31.0, 34.5, 43.0, 44.5, 50.0, 56.5, 64.0)
NORM_READY = (0.9, 6.5, 12.2, 16.0)
FAR_FIRST = (4, 3, 5, 2, 6, 1, 7)
LANES = 128
F32 = jnp.float32
BF16 = jnp.bfloat16


def as_rows(columns):
    n = columns.shape[0]
    if n < LANES:
        columns = jnp.concatenate([columns, jnp.zeros((LANES - n, LANES), F32)], axis=0)
    return columns.T[:8]


def as_columns(rows, n):
    full = jnp.concatenate([rows, jnp.zeros((LANES - 8, LANES), F32)], axis=0)
    return full.T[:n]


def stack_rows(*rows):
    index = lax.broadcasted_iota(jnp.int32, (8, LANES), 0)
    out = jnp.zeros((8, LANES), F32)
    for i, row in enumerate(rows):
        out = jnp.where(index == i, jnp.broadcast_to(row, (8, LANES)), out)
    return out


def combine(tiles):
    top = tiles[0][0:1]
    for t in tiles[1:]:
        top = jnp.maximum(top, t[0:1])
    total = jnp.zeros_like(top)
    picked = jnp.zeros_like(top)
    for t in tiles:
        total = total + t[1:2] * jnp.exp(t[0:1] - top)
        picked = picked + t[2:3]
    return top, total, picked


def kernel(
    ny, nz, nc,
    res_hbm, gain_hbm, w_hbm, act_hbm, beh_hbm, adv_hbm, mask_hbm, clip_hbm,
    loss_ref, head_ref, hid_ref,
    res, gain, w, act, beh, adv, mask, clip, tk,
    sqc, sqz, iny, inx, invc, H, HH, Lo, xs, xr, cs, cr, lg, dcb, dyb, dxb, DL, PB,
    g1, g2, gs, qf, qs, qr, lossz, lsem, ssem, rsem,
):
    grp, seq, voc = lax.axis_index("grp"), lax.axis_index("seq"), lax.axis_index("voc")
    x, y = lax.div(voc, 2), grp * 2 + lax.rem(voc, 2)
    z, c = lax.div(seq, 2), lax.rem(seq, 2)
    oc = 1 - c
    vl, dw = w.shape
    vh = vl // 2
    tp = ROWS * NX
    n_own = res.shape[0]
    half = ny // 2
    left, right, opp = lax.rem(x + 3, NX), lax.rem(x + 1, NX), lax.rem(x + 2, NX)
    order = (x, left, right, opp)

    def dev(x=x, y=y, z=z, c=c):
        return {"grp": lax.div(y, 2), "seq": z * 2 + c, "voc": x * 2 + lax.rem(y, 2)}

    ys = [lax.rem(y + d, ny) for d in FAR_FIRST if d < ny]
    zs = [lax.rem(z + d, nz) for d in FAR_FIRST if d < nz]
    others = [opp, right, left]

    loads = []
    pairs = ((res_hbm, res), (gain_hbm, gain), (w_hbm, w), (act_hbm, act), (beh_hbm, beh),
             (adv_hbm, adv), (mask_hbm, mask), (clip_hbm, clip))
    for i, (src, dst) in enumerate(pairs):
        loads.append(pltpu.make_async_copy(src, dst, lsem.at[i]))
        loads[-1].start()

    started = []

    def send(src, dst, target):
        i = len(started)
        cp = pltpu.make_async_remote_copy(
            src_ref=src, dst_ref=dst, send_sem=ssem.at[i], recv_sem=rsem.at[i],
            device_id=target, device_id_type=pl.DeviceIdType.MESH,
        )
        cp.start()
        started.append(cp)
        return cp

    def arrive(copies):
        for cp in copies:
            cp.wait_recv()

    barrier = pltpu.get_barrier_semaphore()
    partners = (
        [dev(y=t) for t in ys] + [dev(z=t) for t in zs] + [dev(x=t) for t in others] + [dev(c=oc)]
    )
    for p in partners:
        pl.semaphore_signal(barrier, inc=1, device_id=p, device_id_type=pl.DeviceIdType.MESH)

    loads[0].wait()
    sq = res[...].astype(F32)
    sq = sq * sq
    part = sq[:, :LANES]
    for j in range(LANES, dw, LANES):
        part = part + sq[:, j : j + LANES]
    part = jnp.concatenate([part, jnp.zeros((LANES - n_own, LANES), F32)], axis=0)
    sqc[c] = jnp.broadcast_to(jnp.sum(part.T, axis=0, keepdims=True), (8, LANES))
    for k in range(nc):
        H[k, x, y] = res[k * ROWS : (k + 1) * ROWS]
    pl.semaphore_wait(barrier, len(partners))

    gathers = {}

    def gather_y(k):
        gathers[k] = [send(H.at[k, x, y], H.at[k, x, y], dev(y=t)) for t in ys]

    def norm():
        a = [send(sqc.at[c], sqc.at[c], dev(c=oc))]
        gather_y(0)
        for cp in loads[1:]:
            cp.wait()
        n = tk.shape[0]
        vectors = [v[...].astype(F32).reshape(n, LANES) for v in (act, beh, adv, mask, clip)]
        vectors[4] = vectors[4] / 10.0
        for i in range(n):
            tk[i] = stack_rows(*[v[i : i + 1] for v in vectors])
        yield
        arrive(a)
        sqz[z] = sqc[0] + sqc[1]
        a = [send(sqz.at[z], sqz.at[z], dev(z=t)) for t in zs]
        yield
        arrive(a)
        squares = sqz[0]
        for i in range(1, nz):
            squares = squares + sqz[i]
        iny[y] = lax.rsqrt(squares / (dw * nz * 2) + EPSILON)
        a = [send(iny.at[y], iny.at[y], dev(y=t)) for t in ys]
        yield
        arrive(a)
        inx[x] = stack_rows(*[iny[i, 0:1] for i in range(ny)])
        a = [send(inx.at[x], inx.at[x], dev(x=t)) for t in others]
        yield
        arrive(a)
        rows = jnp.concatenate(
            [inx[i] for i in range(NX)] + [jnp.zeros((LANES - 8 * NX, LANES), F32)], axis=0
        )
        columns = rows.T
        for i in range(NX):
            invc[i] = pltpu.roll(columns, (LANES - 8 * i) % LANES, 1) if i else columns

    lane = lax.broadcasted_iota(jnp.int32, (8, LANES), 1)
    losses = []
    first_row = ((grp * NX * 2 + voc) * vl + c * vh).astype(F32)

    def own_tokens(k):
        out = jnp.zeros((8, LANES), F32)
        for i in range(NX):
            block = lax.div(z, 2) * (NX * 2) + i * 2 + lax.rem(z, 2)
            at = block * n_own + k * ROWS
            shift = lax.rem(LANES + i * ROWS - lax.rem(at, LANES), LANES)
            t = pltpu.roll(tk[lax.div(at, LANES)], shift, 1)
            out = jnp.where((lane >= i * ROWS) & (lane < (i + 1) * ROWS), t, out)
        return out

    def terms(k, pos):
        at = order[pos]
        cols = invc[at]
        for j in range(ny):
            unit = H[k, at, j].astype(F32) * cols[k * ROWS : (k + 1) * ROWS, j : j + 1]
            HH[k, at, j] = (unit * gain[...].reshape(1, dw)).astype(BF16)
        h = HH[k, at].reshape(ny * ROWS, dw)
        w_other = w[pl.ds(pl.multiple_of(oc * vh, vh), vh)]
        t = lax.dot_general(h, w_other, (((1,), (1,)), ((), ())), preferred_element_type=F32)
        xs[k, pos] = t.astype(BF16).reshape(ny, ROWS, vh)
        cp = send(xs.at[k, pos], xr.at[k, pos], dev(c=oc))
        w_own = w[pl.ds(pl.multiple_of(c * vh, vh), vh)]
        t = lax.dot_general(h, w_own, (((1,), (1,)), ((), ())), preferred_element_type=F32)
        Lo[k, pos] = t.reshape(ny, ROWS, vh)
        return cp

    def chunk(k):
        last = k == nc - 1
        arrive(gathers[k])
        a = [send(H.at[k, x], H.at[k, x], dev(x=t)) for t in (right, left)]
        if not last:
            gather_y(k + 1)
        yield
        arrive(a)
        low, high = pl.ds(0, half), pl.ds(half, half)
        a = [
            send(H.at[k, left, low], H.at[k, left, low], dev(x=right)),
            send(H.at[k, right, high], H.at[k, right, high], dev(x=left)),
        ]
        yield
        b = [terms(k, pos) for pos in range(NX - 1)]
        yield
        arrive(b)
        near = pl.ds(0, NX - 1)
        b = []
        for t in zs + [z]:
            for pos in range(NX - 1):
                cs[k, t, pos] = (Lo[k, pos, t] + xr[k, pos, t].astype(F32)).astype(BF16)
        for t in zs:
            b.append(send(cs.at[k, t, near], cr.at[k, z, near], dev(z=t)))
        yield
        arrive(a)
        a = [terms(k, NX - 1)]
        yield
        arrive(a)
        far = NX - 1
        for t in zs:
            cs[k, t, far] = (Lo[k, far, t] + xr[k, far, t].astype(F32)).astype(BF16)
            b.append(send(cs.at[k, t, far], cr.at[k, z, far], dev(z=t)))
        yield
        arrive(b)
        for pos in range(NX):
            logits = Lo[k, pos, z] + xr[k, pos, z].astype(F32)
            for t in zs:
                logits = logits + cr[k, t, pos].astype(F32)
            lg[k, order[pos]] = logits
        logits = lg[k].reshape(tp, vh)

        tok = own_tokens(k)
        column = lax.broadcasted_iota(jnp.int32, (tp, vh), 1).astype(F32)
        taken = column == as_columns(tok, tp)[:, 0:1] - first_row
        top = jnp.max(logits, axis=1, keepdims=True)
        total = jnp.sum(jnp.exp(logits - top), axis=1, keepdims=True)
        picked = jnp.sum(jnp.where(taken, logits, 0.0), axis=1, keepdims=True)
        at = lax.broadcasted_iota(jnp.int32, (tp, LANES), 1)
        dcb[k, c] = as_rows(
            jnp.where(at == 0, top, jnp.where(at == 1, total, jnp.where(at == 2, picked, 0.0)))
        )
        a = [send(dcb.at[k, c], dcb.at[k, c], dev(c=oc))]
        yield
        arrive(a)
        dyb[k, y] = stack_rows(*combine([dcb[k, 0], dcb[k, 1]]))
        a = [send(dyb.at[k, y], dyb.at[k, y], dev(y=t)) for t in ys]
        yield
        arrive(a)
        dxb[k, x] = stack_rows(*combine([dyb[k, i] for i in range(ny)]))
        a = [send(dxb.at[k, x], dxb.at[k, x], dev(x=t)) for t in others]
        yield
        arrive(a)
        top, total, picked = combine([dxb[k, i] for i in range(NX)])
        is_own = lane[0:1] < tp
        log_norm = top + jnp.log(jnp.where(is_own, total, 1.0))
        log_prob = picked - log_norm
        ratio = jnp.minimum(jnp.exp(log_prob - tok[1:2]), tok[4:5])
        scaled = tok[3:4] * ratio * tok[2:3]
        losses.append(jnp.sum(jnp.where(is_own, scaled * log_prob, 0.0), axis=1, keepdims=True))
        cols = as_columns(stack_rows(log_norm, GRAD_SCALE * scaled, tok[0:1]), tp)
        taken = column == cols[:, 2:3] - first_row
        softmax = jnp.exp(lg[k].reshape(tp, vh) - cols[:, 0:1])
        dl = (cols[:, 1:2] * (softmax - taken.astype(F32))).astype(BF16)
        for i in range(NX):
            DL[k, c, i, z] = dl[i * ROWS : (i + 1) * ROWS]
        a = [send(DL.at[k, c, :, z], DL.at[k, c, :, z], dev(z=t)) for t in zs]
        if last:
            lossz[z] = jnp.broadcast_to(sum(losses[1:], losses[0]), (8, LANES))
            b = [send(lossz.at[z], lossz.at[z], dev(z=t)) for t in zs]
        yield
        arrive(a)
        a = [send(DL.at[k, c], DL.at[k, c], dev(c=oc))]
        yield
        arrive(a)

        def term(at):
            d0 = DL[k, 0, at].reshape(ny * ROWS, vh)
            d1 = DL[k, 1, at].reshape(ny * ROWS, vh)
            t = jnp.dot(d0, w[0:vh], preferred_element_type=F32)
            t = t + jnp.dot(d1, w[vh:vl], preferred_element_type=F32)
            PB[k, at] = t.astype(BF16).reshape(ny, ROWS, dw)

        term(opp)
        a = [
            send(PB.at[k, opp, low], g1.at[k, 0], dev(x=left)),
            send(PB.at[k, opp, high], g1.at[k, 1], dev(x=right)),
        ]
        term(left)
        b2 = [send(PB.at[k, left, high], g2.at[k, 0, high], dev(x=left))]
        term(right)
        b2.append(send(PB.at[k, right, low], g2.at[k, 1, low], dev(x=right)))
        term(x)
        yield
        arrive(a)
        gs[k, 0] = (PB[k, left, low].astype(F32) + g1[k, 0].astype(F32)).astype(BF16)
        b2.append(send(gs.at[k, 0], g2.at[k, 0, low], dev(x=left)))
        gs[k, 1] = (PB[k, right, high].astype(F32) + g1[k, 1].astype(F32)).astype(BF16)
        b2.append(send(gs.at[k, 1], g2.at[k, 1, high], dev(x=right)))
        if last:
            h_all = HH[...].reshape(nc * NX * ny * ROWS, dw)
            for i in range(2):
                d_all = DL[:, i].reshape(nc * NX * ny * ROWS, vh)
                t = lax.dot_general(
                    d_all, h_all, (((0,), (0,)), ((), ())), preferred_element_type=F32
                )
                head_ref[i * vh : (i + 1) * vh, :] = t.astype(BF16)
        yield
        arrive(b2)
        for t in ys + [y]:
            q = PB[k, x, t].astype(F32) + g2[k, 0, t].astype(F32) + g2[k, 1, t].astype(F32)
            qf[k, t] = q
            qs[k, t] = q.astype(BF16)
        a = [send(qs.at[k, t], qr.at[k, y], dev(y=t)) for t in ys]
        yield
        arrive(a)
        q = qf[k, y]
        for t in ys:
            q = q + qr[k, t].astype(F32)
        hid_ref[k * ROWS : (k + 1) * ROWS, :] = q
        if last:
            arrive(b)
            loss = lossz[0]
            for i in range(1, nz):
                loss = loss + lossz[i]
            loss_ref[0, 0] = jnp.max(loss[0:1]) * (-1.0 / (n_own * NX * ny))

    plan = [(t, -1) for t in (0.0,) + NORM_READY]
    plan += [(t + STAGGER * k, k) for k in range(nc) for t in READY]
    runs = {-1: norm()}
    runs.update((k, chunk(k)) for k in range(nc))
    for _, k in sorted(plan):
        next(runs[k], None)
    for cp in started:
        cp.wait_send()


def per_device(mesh_sizes, residual, norm_gain, head_weight, actions, behavior_logp, advantages, decision_mask, clip_tenths):
    n_grp, n_seq, n_voc = mesh_sizes
    ny, nz = n_grp * 2, n_seq // 2
    n_own, dw = residual.shape
    vl = head_weight.shape[0]
    tokens = actions.shape[0]
    nc = n_own // ROWS
    vh = vl // 2

    per_chunk = 4 * (ny - 1) + 3 * (nz - 1) + 2 + 2 + NX + 1 + (NX - 1) + 1 + 6
    n_sends = 1 + (nz - 1) + (ny - 1) + (NX - 1) + nc * per_chunk + nz - 1
    any_space = pl.BlockSpec(memory_space=pl.ANY)
    vm = pl.BlockSpec(memory_space=pltpu.VMEM)
    tile = (8, LANES)
    loss, head_grad, hidden_grad = pl.pallas_call(
        functools.partial(kernel, ny, nz, nc),
        out_shape=(
            jax.ShapeDtypeStruct((1, 1), F32),
            jax.ShapeDtypeStruct((vl, dw), BF16),
            jax.ShapeDtypeStruct((n_own, dw), F32),
        ),
        in_specs=[any_space] * 8,
        out_specs=(pl.BlockSpec(memory_space=pltpu.SMEM), vm, vm),
        scratch_shapes=[
            pltpu.VMEM((n_own, dw), BF16),
            pltpu.VMEM((dw,), F32),
            pltpu.VMEM((vl, dw), BF16),
            pltpu.VMEM((tokens,), jnp.int32),
            pltpu.VMEM((tokens,), F32),
            pltpu.VMEM((tokens,), F32),
            pltpu.VMEM((tokens,), jnp.int32),
            pltpu.VMEM((tokens,), jnp.int32),
            pltpu.VMEM((tokens // LANES,) + tile, F32),
            pltpu.VMEM((2,) + tile, F32),
            pltpu.VMEM((nz,) + tile, F32),
            pltpu.VMEM((ny,) + tile, F32),
            pltpu.VMEM((NX,) + tile, F32),
            pltpu.VMEM((NX, LANES, LANES), F32),
            pltpu.VMEM((nc, NX, ny, ROWS, dw), BF16),
            pltpu.VMEM((nc, NX, ny, ROWS, dw), BF16),
            pltpu.VMEM((nc, NX, ny, ROWS, vh), F32),
            pltpu.VMEM((nc, NX, ny, ROWS, vh), BF16),
            pltpu.VMEM((nc, NX, ny, ROWS, vh), BF16),
            pltpu.VMEM((nc, nz, NX, ROWS, vh), BF16),
            pltpu.VMEM((nc, nz, NX, ROWS, vh), BF16),
            pltpu.VMEM((nc, NX, ROWS, vh), F32),
            pltpu.VMEM((nc, 2) + tile, F32),
            pltpu.VMEM((nc, ny) + tile, F32),
            pltpu.VMEM((nc, NX) + tile, F32),
            pltpu.VMEM((nc, 2, NX, ny, ROWS, vh), BF16),
            pltpu.VMEM((nc, NX, ny, ROWS, dw), BF16),
            pltpu.VMEM((nc, 2, ny // 2, ROWS, dw), BF16),
            pltpu.VMEM((nc, 2, ny, ROWS, dw), BF16),
            pltpu.VMEM((nc, 2, ny // 2, ROWS, dw), BF16),
            pltpu.VMEM((nc, ny, ROWS, dw), F32),
            pltpu.VMEM((nc, ny, ROWS, dw), BF16),
            pltpu.VMEM((nc, ny, ROWS, dw), BF16),
            pltpu.VMEM((nz,) + tile, F32),
            pltpu.SemaphoreType.DMA((8,)),
            pltpu.SemaphoreType.DMA((n_sends,)),
            pltpu.SemaphoreType.DMA((n_sends,)),
        ],
        compiler_params=pltpu.CompilerParams(
            collective_id=0, has_side_effects=True, vmem_limit_bytes=60 * 2**20
        ),
    )(residual, norm_gain, head_weight, actions, behavior_logp, advantages, decision_mask, clip_tenths)
    return loss.reshape(()), head_grad, hidden_grad


def solution(mesh):
    sizes = (mesh.shape["grp"], mesh.shape["seq"], mesh.shape["voc"])
    split = P(("grp", "voc"), "seq")
    return jax.shard_map(
        functools.partial(per_device, sizes),
        mesh=mesh,
        in_specs=(split, P("seq"), split, P(), P(), P(), P(), P()),
        out_specs=(P(), split, split),
        check_vma=False,
    )
```

```python
import functools

import jax
import jax.numpy as jnp
from jax import lax
from jax.experimental import pallas as pl
from jax.experimental.pallas import tpu as pltpu
from jax.sharding import PartitionSpec as P

EPSILON = 1e-05
GRAD_SCALE = 8.0
NX = 4
ROWS = 16
NORM, GATHER, HEAD = -1, 3, 4
PLAN = (
    -1, -1, 0, -1, 3, 3, -1, 0, 1, -1, 0, 2, 0, 0, 1, 1, 0, 1, 2, 2, 1, 0, 1, 0,
    2, 2, 2, 1, 0, 1, 0, 2, 1, 2, 0, 0, 1, 0, 2, 0, 0, 1, 2, 1, 1, 1, 2, 0,
    2, 1, 2, 2, 2, 0, 1, 2, 4, 1, 2,
)
FAR_FIRST = (4, 3, 5, 2, 6, 1, 7)
LANES = 128
F32 = jnp.float32
BF16 = jnp.bfloat16


def as_rows(columns):
    n = columns.shape[0]
    if n < LANES:
        columns = jnp.concatenate([columns, jnp.zeros((LANES - n, LANES), F32)], axis=0)
    return columns.T[:8]


def as_columns(rows, n):
    full = jnp.concatenate([rows, jnp.zeros((LANES - 8, LANES), F32)], axis=0)
    return full.T[:n]


def stack_rows(*rows):
    index = lax.broadcasted_iota(jnp.int32, (8, LANES), 0)
    out = jnp.zeros((8, LANES), F32)
    for i, row in enumerate(rows):
        out = jnp.where(index == i, jnp.broadcast_to(row, (8, LANES)), out)
    return out


def combine(tiles):
    top = tiles[0][0:1]
    for t in tiles[1:]:
        top = jnp.maximum(top, t[0:1])
    total = jnp.zeros_like(top)
    picked = jnp.zeros_like(top)
    for t in tiles:
        total = total + t[1:2] * jnp.exp(t[0:1] - top)
        picked = picked + t[2:3]
    return top, total, picked


def kernel(
    ny, nz, nc,
    res_hbm, gain_hbm, w_hbm, act_hbm, beh_hbm, adv_hbm, mask_hbm, clip_hbm,
    loss_ref, head_ref, hid_ref,
    res, gain, w, act, beh, adv, mask, clip, tk,
    sqc, sqz, iny, inx, invc, H, HH, Lo, xs, xr, cs, cr, lg, dcb, dyb, dxb, dlx, DL, PB,
    g1, g2, gs, qf, qs, qr, lossz, lsem, ssem, rsem,
):
    grp, seq, voc = lax.axis_index("grp"), lax.axis_index("seq"), lax.axis_index("voc")
    x, y = lax.div(voc, 2), grp * 2 + lax.rem(voc, 2)
    z, c = lax.div(seq, 2), lax.rem(seq, 2)
    oc = 1 - c
    vl, dw = w.shape
    vh = vl // 2
    tp = ROWS * NX
    n_own = res.shape[0]
    half = ny // 2
    left, right, opp = lax.rem(x + 3, NX), lax.rem(x + 1, NX), lax.rem(x + 2, NX)
    order = (x, left, right, opp)

    def dev(x=x, y=y, z=z, c=c):
        return {"grp": lax.div(y, 2), "seq": z * 2 + c, "voc": x * 2 + lax.rem(y, 2)}

    ys = [lax.rem(y + d, ny) for d in FAR_FIRST if d < ny]
    zs = [lax.rem(z + d, nz) for d in FAR_FIRST if d < nz]
    others = [opp, right, left]

    loads = []
    pairs = ((res_hbm, res), (gain_hbm, gain), (w_hbm, w), (act_hbm, act), (beh_hbm, beh),
             (adv_hbm, adv), (mask_hbm, mask), (clip_hbm, clip))
    for i, (src, dst) in enumerate(pairs):
        loads.append(pltpu.make_async_copy(src, dst, lsem.at[i]))
        loads[-1].start()

    started = []

    def send(src, dst, target):
        i = len(started)
        cp = pltpu.make_async_remote_copy(
            src_ref=src, dst_ref=dst, send_sem=ssem.at[i], recv_sem=rsem.at[i],
            device_id=target, device_id_type=pl.DeviceIdType.MESH,
        )
        cp.start()
        started.append(cp)
        return cp

    def arrive(copies):
        for cp in copies:
            cp.wait_recv()

    barrier = pltpu.get_barrier_semaphore()
    partners = (
        [dev(y=t) for t in ys] + [dev(z=t) for t in zs] + [dev(x=t) for t in others] + [dev(c=oc)]
    )
    for p in partners:
        pl.semaphore_signal(barrier, inc=1, device_id=p, device_id_type=pl.DeviceIdType.MESH)

    loads[0].wait()
    sq = res[...].astype(F32)
    sq = sq * sq
    part = sq[:, :LANES]
    for j in range(LANES, dw, LANES):
        part = part + sq[:, j : j + LANES]
    part = jnp.concatenate([part, jnp.zeros((LANES - n_own, LANES), F32)], axis=0)
    sqc[c] = jnp.broadcast_to(jnp.sum(part.T, axis=0, keepdims=True), (8, LANES))
    for k in range(nc):
        H[k, x, y] = res[k * ROWS : (k + 1) * ROWS]
    pl.semaphore_wait(barrier, len(partners))

    gathers = {}

    def gather_y(k):
        gathers[k] = [send(H.at[k, x, y], H.at[k, x, y], dev(y=t)) for t in ys]

    def norm():
        a = [send(sqc.at[c], sqc.at[c], dev(c=oc))]
        gather_y(0)
        for cp in loads[1:]:
            cp.wait()
        n = tk.shape[0]
        vectors = [v[...].astype(F32).reshape(n, LANES) for v in (act, beh, adv, mask, clip)]
        vectors[4] = vectors[4] / 10.0
        for i in range(n):
            tk[i] = stack_rows(*[v[i : i + 1] for v in vectors])
        yield
        arrive(a)
        sqz[z] = sqc[0] + sqc[1]
        a = [send(sqz.at[z], sqz.at[z], dev(z=t)) for t in zs]
        yield
        arrive(a)
        squares = sqz[0]
        for i in range(1, nz):
            squares = squares + sqz[i]
        iny[y] = lax.rsqrt(squares / (dw * nz * 2) + EPSILON)
        a = [send(iny.at[y], iny.at[y], dev(y=t)) for t in ys]
        yield
        arrive(a)
        inx[x] = stack_rows(*[iny[i, 0:1] for i in range(ny)])
        a = [send(inx.at[x], inx.at[x], dev(x=t)) for t in others]
        yield
        arrive(a)
        rows = jnp.concatenate(
            [inx[i] for i in range(NX)] + [jnp.zeros((LANES - 8 * NX, LANES), F32)], axis=0
        )
        columns = rows.T
        for i in range(NX):
            invc[i] = pltpu.roll(columns, (LANES - 8 * i) % LANES, 1) if i else columns

    lane = lax.broadcasted_iota(jnp.int32, (8, LANES), 1)
    losses = []
    first_row = ((grp * NX * 2 + voc) * vl + c * vh).astype(F32)

    def own_tokens(k):
        out = jnp.zeros((8, LANES), F32)
        for i in range(NX):
            block = lax.div(z, 2) * (NX * 2) + i * 2 + lax.rem(z, 2)
            at = block * n_own + k * ROWS
            shift = lax.rem(LANES + i * ROWS - lax.rem(at, LANES), LANES)
            t = pltpu.roll(tk[lax.div(at, LANES)], shift, 1)
            out = jnp.where((lane >= i * ROWS) & (lane < (i + 1) * ROWS), t, out)
        return out

    def terms(k, pos):
        at = order[pos]
        cols = invc[at]
        for j in range(ny):
            unit = H[k, at, j].astype(F32) * cols[k * ROWS : (k + 1) * ROWS, j : j + 1]
            HH[k, pos, j] = (unit * gain[...].reshape(1, dw)).astype(BF16)
        h = HH[k, pos].reshape(ny * ROWS, dw)
        w_other = w[pl.ds(pl.multiple_of(oc * vh, vh), vh)]
        t = lax.dot_general(h, w_other, (((1,), (1,)), ((), ())), preferred_element_type=F32)
        xs[k, pos] = t.astype(BF16).reshape(ny, ROWS, vh)
        cp = send(xs.at[k, pos], xr.at[k, pos], dev(c=oc))
        w_own = w[pl.ds(pl.multiple_of(c * vh, vh), vh)]
        t = lax.dot_general(h, w_own, (((1,), (1,)), ((), ())), preferred_element_type=F32)
        Lo[k, pos] = t.reshape(ny, ROWS, vh)
        return cp

    def chunk(k):
        last = k == nc - 1
        arrive(gathers[k])
        a = [send(H.at[k, x], H.at[k, x], dev(x=t)) for t in (right, left)]
        yield
        arrive(a)
        low, high = pl.ds(0, half), pl.ds(half, half)
        a = [
            send(H.at[k, left, low], H.at[k, left, low], dev(x=right)),
            send(H.at[k, right, high], H.at[k, right, high], dev(x=left)),
        ]
        yield
        b = [terms(k, pos) for pos in range(NX - 1)]
        yield
        arrive(b)
        near = pl.ds(0, NX - 1)
        b = []
        for t in zs + [z]:
            for pos in range(NX - 1):
                cs[k, t, pos] = (Lo[k, pos, t] + xr[k, pos, t].astype(F32)).astype(BF16)
        for t in zs:
            b.append(send(cs.at[k, t, near], cr.at[k, z, near], dev(z=t)))
        yield
        arrive(a)
        a = [terms(k, NX - 1)]
        yield
        arrive(a)
        far = NX - 1
        for t in zs:
            cs[k, t, far] = (Lo[k, far, t] + xr[k, far, t].astype(F32)).astype(BF16)
            b.append(send(cs.at[k, t, far], cr.at[k, z, far], dev(z=t)))
        yield
        arrive(b)
        for pos in range(NX):
            logits = Lo[k, pos, z] + xr[k, pos, z].astype(F32)
            for t in zs:
                logits = logits + cr[k, t, pos].astype(F32)
            lg[k, order[pos]] = logits
        logits = lg[k].reshape(tp, vh)

        tok = own_tokens(k)
        column = lax.broadcasted_iota(jnp.int32, (tp, vh), 1).astype(F32)
        taken = column == as_columns(tok, tp)[:, 0:1] - first_row
        top = jnp.max(logits, axis=1, keepdims=True)
        total = jnp.sum(jnp.exp(logits - top), axis=1, keepdims=True)
        picked = jnp.sum(jnp.where(taken, logits, 0.0), axis=1, keepdims=True)
        at = lax.broadcasted_iota(jnp.int32, (tp, LANES), 1)
        dcb[k, c] = as_rows(
            jnp.where(at == 0, top, jnp.where(at == 1, total, jnp.where(at == 2, picked, 0.0)))
        )
        a = [send(dcb.at[k, c], dcb.at[k, c], dev(c=oc))]
        yield
        arrive(a)
        dyb[k, y] = stack_rows(*combine([dcb[k, 0], dcb[k, 1]]))
        a = [send(dyb.at[k, y], dyb.at[k, y], dev(y=t)) for t in ys]
        yield
        arrive(a)
        dxb[k, x] = stack_rows(*combine([dyb[k, i] for i in range(ny)]))
        a = [send(dxb.at[k, x], dxb.at[k, x], dev(x=t)) for t in others]
        yield
        arrive(a)
        top, total, picked = combine([dxb[k, i] for i in range(NX)])
        is_own = lane[0:1] < tp
        log_norm = top + jnp.log(jnp.where(is_own, total, 1.0))
        log_prob = picked - log_norm
        ratio = jnp.minimum(jnp.exp(log_prob - tok[1:2]), tok[4:5])
        scaled = tok[3:4] * ratio * tok[2:3]
        losses.append(jnp.sum(jnp.where(is_own, scaled * log_prob, 0.0), axis=1, keepdims=True))
        cols = as_columns(stack_rows(log_norm, GRAD_SCALE * scaled, tok[0:1]), tp)
        taken = column == cols[:, 2:3] - first_row
        softmax = jnp.exp(lg[k].reshape(tp, vh) - cols[:, 0:1])
        dl = (cols[:, 1:2] * (softmax - taken.astype(F32))).astype(BF16)
        for i in range(NX):
            dlx[k, i] = dl[i * ROWS : (i + 1) * ROWS]
        for pos in range(NX):
            DL[k, c, pos, z] = dlx[k, order[pos]]
        far, near = NX - 1, pl.ds(0, NX - 1)
        a = [send(DL.at[k, c, far, z], DL.at[k, c, far, z], dev(z=t)) for t in zs]
        d = [send(DL.at[k, c, near, z], DL.at[k, c, near, z], dev(z=t)) for t in zs]
        if last:
            lossz[z] = jnp.broadcast_to(sum(losses[1:], losses[0]), (8, LANES))
            b = [send(lossz.at[z], lossz.at[z], dev(z=t)) for t in zs]
        yield
        arrive(a)
        a = [send(DL.at[k, c, far], DL.at[k, c, far], dev(c=oc))]
        yield
        arrive(a)

        def term(pos):
            d0 = DL[k, 0, pos].reshape(ny * ROWS, vh)
            d1 = DL[k, 1, pos].reshape(ny * ROWS, vh)
            t = jnp.dot(d0, w[0:vh], preferred_element_type=F32)
            t = t + jnp.dot(d1, w[vh:vl], preferred_element_type=F32)
            PB[k, pos] = t.astype(BF16).reshape(ny, ROWS, dw)

        term(3)
        a = [
            send(PB.at[k, 3, low], g1.at[k, 0], dev(x=left)),
            send(PB.at[k, 3, high], g1.at[k, 1], dev(x=right)),
        ]
        yield
        arrive(d)
        d = [send(DL.at[k, c, near], DL.at[k, c, near], dev(c=oc))]
        yield
        arrive(d)
        term(1)
        b2 = [send(PB.at[k, 1, high], g2.at[k, 0, high], dev(x=left))]
        term(2)
        b2.append(send(PB.at[k, 2, low], g2.at[k, 1, low], dev(x=right)))
        term(0)
        yield
        arrive(a)
        gs[k, 0] = (PB[k, 1, low].astype(F32) + g1[k, 0].astype(F32)).astype(BF16)
        b2.append(send(gs.at[k, 0], g2.at[k, 0, low], dev(x=left)))
        gs[k, 1] = (PB[k, 2, high].astype(F32) + g1[k, 1].astype(F32)).astype(BF16)
        b2.append(send(gs.at[k, 1], g2.at[k, 1, high], dev(x=right)))
        yield
        arrive(b2)
        for t in ys + [y]:
            q = PB[k, 0, t].astype(F32) + g2[k, 0, t].astype(F32) + g2[k, 1, t].astype(F32)
            qf[k, t] = q
            qs[k, t] = q.astype(BF16)
        a = [send(qs.at[k, t], qr.at[k, y], dev(y=t)) for t in ys]
        yield
        arrive(a)
        q = qf[k, y]
        for t in ys:
            q = q + qr[k, t].astype(F32)
        hid_ref[k * ROWS : (k + 1) * ROWS, :] = q
        if last:
            arrive(b)
            loss = lossz[0]
            for i in range(1, nz):
                loss = loss + lossz[i]
            loss_ref[0, 0] = jnp.max(loss[0:1]) * (-1.0 / (n_own * NX * ny))

    def gather():
        for k in range(1, nc):
            gather_y(k)
            yield

    def head():
        h_all = HH[...].reshape(nc * NX * ny * ROWS, dw)
        for i in range(2):
            d_all = DL[:, i].reshape(nc * NX * ny * ROWS, vh)
            t = lax.dot_general(d_all, h_all, (((0,), (0,)), ((), ())), preferred_element_type=F32)
            head_ref[i * vh : (i + 1) * vh, :] = t.astype(BF16)
        yield

    runs = {NORM: norm(), GATHER: gather(), HEAD: head()}
    runs.update((k, chunk(k)) for k in range(nc))
    for step in PLAN:
        next(runs[step], None)
    for cp in started:
        cp.wait_send()


def per_device(mesh_sizes, residual, norm_gain, head_weight, actions, behavior_logp, advantages, decision_mask, clip_tenths):
    n_grp, n_seq, n_voc = mesh_sizes
    ny, nz = n_grp * 2, n_seq // 2
    n_own, dw = residual.shape
    vl = head_weight.shape[0]
    tokens = actions.shape[0]
    nc = n_own // ROWS
    vh = vl // 2

    per_chunk = 3 * (ny - 1) + 4 * (nz - 1) + 2 + 2 + NX + 1 + (NX - 1) + 2 + 6
    n_sends = 1 + (nz - 1) + (ny - 1) + (NX - 1) + nc * per_chunk + nz - 1
    any_space = pl.BlockSpec(memory_space=pl.ANY)
    vm = pl.BlockSpec(memory_space=pltpu.VMEM)
    tile = (8, LANES)
    loss, head_grad, hidden_grad = pl.pallas_call(
        functools.partial(kernel, ny, nz, nc),
        out_shape=(
            jax.ShapeDtypeStruct((1, 1), F32),
            jax.ShapeDtypeStruct((vl, dw), BF16),
            jax.ShapeDtypeStruct((n_own, dw), F32),
        ),
        in_specs=[any_space] * 8,
        out_specs=(pl.BlockSpec(memory_space=pltpu.SMEM), vm, vm),
        scratch_shapes=[
            pltpu.VMEM((n_own, dw), BF16),
            pltpu.VMEM((dw,), F32),
            pltpu.VMEM((vl, dw), BF16),
            pltpu.VMEM((tokens,), jnp.int32),
            pltpu.VMEM((tokens,), F32),
            pltpu.VMEM((tokens,), F32),
            pltpu.VMEM((tokens,), jnp.int32),
            pltpu.VMEM((tokens,), jnp.int32),
            pltpu.VMEM((tokens // LANES,) + tile, F32),
            pltpu.VMEM((2,) + tile, F32),
            pltpu.VMEM((nz,) + tile, F32),
            pltpu.VMEM((ny,) + tile, F32),
            pltpu.VMEM((NX,) + tile, F32),
            pltpu.VMEM((NX, LANES, LANES), F32),
            pltpu.VMEM((nc, NX, ny, ROWS, dw), BF16),
            pltpu.VMEM((nc, NX, ny, ROWS, dw), BF16),
            pltpu.VMEM((nc, NX, ny, ROWS, vh), F32),
            pltpu.VMEM((nc, NX, ny, ROWS, vh), BF16),
            pltpu.VMEM((nc, NX, ny, ROWS, vh), BF16),
            pltpu.VMEM((nc, nz, NX, ROWS, vh), BF16),
            pltpu.VMEM((nc, nz, NX, ROWS, vh), BF16),
            pltpu.VMEM((nc, NX, ROWS, vh), F32),
            pltpu.VMEM((nc, 2) + tile, F32),
            pltpu.VMEM((nc, ny) + tile, F32),
            pltpu.VMEM((nc, NX) + tile, F32),
            pltpu.VMEM((nc, NX, ROWS, vh), BF16),
            pltpu.VMEM((nc, 2, NX, ny, ROWS, vh), BF16),
            pltpu.VMEM((nc, NX, ny, ROWS, dw), BF16),
            pltpu.VMEM((nc, 2, ny // 2, ROWS, dw), BF16),
            pltpu.VMEM((nc, 2, ny, ROWS, dw), BF16),
            pltpu.VMEM((nc, 2, ny // 2, ROWS, dw), BF16),
            pltpu.VMEM((nc, ny, ROWS, dw), F32),
            pltpu.VMEM((nc, ny, ROWS, dw), BF16),
            pltpu.VMEM((nc, ny, ROWS, dw), BF16),
            pltpu.VMEM((nz,) + tile, F32),
            pltpu.SemaphoreType.DMA((8,)),
            pltpu.SemaphoreType.DMA((n_sends,)),
            pltpu.SemaphoreType.DMA((n_sends,)),
        ],
        compiler_params=pltpu.CompilerParams(
            collective_id=0, has_side_effects=True, vmem_limit_bytes=60 * 2**20
        ),
    )(residual, norm_gain, head_weight, actions, behavior_logp, advantages, decision_mask, clip_tenths)
    return loss.reshape(()), head_grad, hidden_grad


def solution(mesh):
    sizes = (mesh.shape["grp"], mesh.shape["seq"], mesh.shape["voc"])
    split = P(("grp", "voc"), "seq")
    return jax.shard_map(
        functools.partial(per_device, sizes),
        mesh=mesh,
        in_specs=(split, P("seq"), split, P(), P(), P(), P(), P()),
        out_specs=(P(), split, split),
        check_vma=False,
    )
```

```python
import functools

import jax
import jax.numpy as jnp
from jax import lax
from jax.experimental import pallas as pl
from jax.experimental.pallas import tpu as pltpu
from jax.sharding import PartitionSpec as P

EPSILON = 1e-05
GRAD_SCALE = 8.0
NX = 4
ROWS = 16
NORM, GATHER, HEAD = -1, 3, 4
PLAN = (
    -1, -1, 0, -1, 3, 3, -1, 0, 1, -1, 0, 0, 0, 1, 2, 0, 1, 1, 1, 0, 1, 0, 2, 2,
    2, 1, 0, 1, 2, 2, 0, 1, 2, 2, 0, 1, 0, 0, 2, 0, 1, 1, 2, 0, 1, 1, 2, 1,
    2, 0, 2, 2, 1, 2, 4, 2, 0, 2, 1, 2,
)
FAR_FIRST = (4, 3, 5, 2, 6, 1, 7)
LANES = 128
F32 = jnp.float32
BF16 = jnp.bfloat16


def as_rows(columns):
    n = columns.shape[0]
    if n < LANES:
        columns = jnp.concatenate([columns, jnp.zeros((LANES - n, LANES), F32)], axis=0)
    return columns.T[:8]


def as_columns(rows, n):
    full = jnp.concatenate([rows, jnp.zeros((LANES - 8, LANES), F32)], axis=0)
    return full.T[:n]


def stack_rows(*rows):
    index = lax.broadcasted_iota(jnp.int32, (8, LANES), 0)
    out = jnp.zeros((8, LANES), F32)
    for i, row in enumerate(rows):
        out = jnp.where(index == i, jnp.broadcast_to(row, (8, LANES)), out)
    return out


def combine(tiles):
    top = tiles[0][0:1]
    for t in tiles[1:]:
        top = jnp.maximum(top, t[0:1])
    total = jnp.zeros_like(top)
    picked = jnp.zeros_like(top)
    for t in tiles:
        total = total + t[1:2] * jnp.exp(t[0:1] - top)
        picked = picked + t[2:3]
    return top, total, picked


def kernel(
    ny, nz, nc,
    res_hbm, gain_hbm, w_hbm, act_hbm, beh_hbm, adv_hbm, mask_hbm, clip_hbm,
    loss_ref, head_ref, hid_ref,
    res, gain, w, act, beh, adv, mask, clip, tk,
    sqc, sqz, iny, inx, invc, H, HH, Lo, xs, xr, cs, cr, lg, dcb, dyb, dxb, dlx, DL, PB,
    g1, g2, gs, qf, qs, qr, lossz, lsem, ssem, rsem,
):
    grp, seq, voc = lax.axis_index("grp"), lax.axis_index("seq"), lax.axis_index("voc")
    x, y = lax.div(voc, 2), grp * 2 + lax.rem(voc, 2)
    z, c = lax.div(seq, 2), lax.rem(seq, 2)
    oc = 1 - c
    vl, dw = w.shape
    vh = vl // 2
    tp = ROWS * NX
    n_own = res.shape[0]
    half = ny // 2
    left, right, opp = lax.rem(x + 3, NX), lax.rem(x + 1, NX), lax.rem(x + 2, NX)
    order = (x, left, right, opp)

    def dev(x=x, y=y, z=z, c=c):
        return {"grp": lax.div(y, 2), "seq": z * 2 + c, "voc": x * 2 + lax.rem(y, 2)}

    ys = [lax.rem(y + d, ny) for d in FAR_FIRST if d < ny]
    zs = [lax.rem(z + d, nz) for d in FAR_FIRST if d < nz]
    others = [opp, right, left]

    loads = []
    pairs = ((res_hbm, res), (gain_hbm, gain), (w_hbm, w), (act_hbm, act), (beh_hbm, beh),
             (adv_hbm, adv), (mask_hbm, mask), (clip_hbm, clip))
    for i, (src, dst) in enumerate(pairs):
        loads.append(pltpu.make_async_copy(src, dst, lsem.at[i]))
        loads[-1].start()

    started = []

    def send(src, dst, target):
        i = len(started)
        cp = pltpu.make_async_remote_copy(
            src_ref=src, dst_ref=dst, send_sem=ssem.at[i], recv_sem=rsem.at[i],
            device_id=target, device_id_type=pl.DeviceIdType.MESH,
        )
        cp.start()
        started.append(cp)
        return cp

    def arrive(copies):
        for cp in copies:
            cp.wait_recv()

    barrier = pltpu.get_barrier_semaphore()
    partners = (
        [dev(y=t) for t in ys] + [dev(z=t) for t in zs] + [dev(x=t) for t in others] + [dev(c=oc)]
    )
    for p in partners:
        pl.semaphore_signal(barrier, inc=1, device_id=p, device_id_type=pl.DeviceIdType.MESH)

    loads[0].wait()
    sq = res[...].astype(F32)
    sq = sq * sq
    part = sq[:, :LANES]
    for j in range(LANES, dw, LANES):
        part = part + sq[:, j : j + LANES]
    part = jnp.concatenate([part, jnp.zeros((LANES - n_own, LANES), F32)], axis=0)
    sqc[c] = jnp.broadcast_to(jnp.sum(part.T, axis=0, keepdims=True), (8, LANES))
    for k in range(nc):
        H[k, x, y] = res[k * ROWS : (k + 1) * ROWS]
    pl.semaphore_wait(barrier, len(partners))

    gathers = {}

    def gather_y(k):
        gathers[k] = [send(H.at[k, x, y], H.at[k, x, y], dev(y=t)) for t in ys]

    def norm():
        a = [send(sqc.at[c], sqc.at[c], dev(c=oc))]
        gather_y(0)
        for cp in loads[1:]:
            cp.wait()
        n = tk.shape[0]
        vectors = [v[...].astype(F32).reshape(n, LANES) for v in (act, beh, adv, mask, clip)]
        vectors[4] = vectors[4] / 10.0
        for i in range(n):
            tk[i] = stack_rows(*[v[i : i + 1] for v in vectors])
        yield
        arrive(a)
        sqz[z] = sqc[0] + sqc[1]
        a = [send(sqz.at[z], sqz.at[z], dev(z=t)) for t in zs]
        yield
        arrive(a)
        squares = sqz[0]
        for i in range(1, nz):
            squares = squares + sqz[i]
        iny[y] = lax.rsqrt(squares / (dw * nz * 2) + EPSILON)
        a = [send(iny.at[y], iny.at[y], dev(y=t)) for t in ys]
        yield
        arrive(a)
        inx[x] = stack_rows(*[iny[i, 0:1] for i in range(ny)])
        a = [send(inx.at[x], inx.at[x], dev(x=t)) for t in others]
        yield
        arrive(a)
        rows = jnp.concatenate(
            [inx[i] for i in range(NX)] + [jnp.zeros((LANES - 8 * NX, LANES), F32)], axis=0
        )
        columns = rows.T
        for i in range(NX):
            invc[i] = pltpu.roll(columns, (LANES - 8 * i) % LANES, 1) if i else columns

    lane = lax.broadcasted_iota(jnp.int32, (8, LANES), 1)
    losses = []
    first_row = ((grp * NX * 2 + voc) * vl + c * vh).astype(F32)

    def own_tokens(k):
        out = jnp.zeros((8, LANES), F32)
        for i in range(NX):
            block = lax.div(z, 2) * (NX * 2) + i * 2 + lax.rem(z, 2)
            at = block * n_own + k * ROWS
            shift = lax.rem(LANES + i * ROWS - lax.rem(at, LANES), LANES)
            t = pltpu.roll(tk[lax.div(at, LANES)], shift, 1)
            out = jnp.where((lane >= i * ROWS) & (lane < (i + 1) * ROWS), t, out)
        return out

    def terms(k, pos):
        at = order[pos]
        cols = invc[at]
        for j in range(ny):
            unit = H[k, at, j].astype(F32) * cols[k * ROWS : (k + 1) * ROWS, j : j + 1]
            HH[k, pos, j] = (unit * gain[...].reshape(1, dw)).astype(BF16)
        h = HH[k, pos].reshape(ny * ROWS, dw)
        w_other = w[pl.ds(pl.multiple_of(oc * vh, vh), vh)]
        t = lax.dot_general(h, w_other, (((1,), (1,)), ((), ())), preferred_element_type=F32)
        xs[k, pos] = t.astype(BF16).reshape(ny, ROWS, vh)
        cp = send(xs.at[k, pos], xr.at[k, pos], dev(c=oc))
        w_own = w[pl.ds(pl.multiple_of(c * vh, vh), vh)]
        t = lax.dot_general(h, w_own, (((1,), (1,)), ((), ())), preferred_element_type=F32)
        Lo[k, pos] = t.reshape(ny, ROWS, vh)
        return cp

    def chunk(k):
        last = k == nc - 1
        arrive(gathers[k])
        a = [send(H.at[k, x], H.at[k, x], dev(x=t)) for t in (right, left)]
        yield
        arrive(a)
        low, high = pl.ds(0, half), pl.ds(half, half)
        a = [
            send(H.at[k, left, low], H.at[k, left, low], dev(x=right)),
            send(H.at[k, right, high], H.at[k, right, high], dev(x=left)),
        ]
        yield
        b = [terms(k, pos) for pos in range(NX - 1)]
        yield
        arrive(b)
        near = pl.ds(0, NX - 1)
        b = []
        for t in zs:
            for pos in range(NX - 1):
                cs[k, t, pos] = (Lo[k, pos, t] + xr[k, pos, t].astype(F32)).astype(BF16)
            b.append(send(cs.at[k, t, near], cr.at[k, z, near], dev(z=t)))
        yield
        arrive(a)
        a = [terms(k, NX - 1)]
        yield
        arrive(a)
        far = NX - 1
        for t in zs:
            cs[k, t, far] = (Lo[k, far, t] + xr[k, far, t].astype(F32)).astype(BF16)
            b.append(send(cs.at[k, t, far], cr.at[k, z, far], dev(z=t)))
        yield
        arrive(b)
        for pos in range(NX):
            logits = Lo[k, pos, z] + xr[k, pos, z].astype(F32)
            for t in zs:
                logits = logits + cr[k, t, pos].astype(F32)
            lg[k, order[pos]] = logits
        logits = lg[k].reshape(tp, vh)

        tok = own_tokens(k)
        column = lax.broadcasted_iota(jnp.int32, (tp, vh), 1).astype(F32)
        taken = column == as_columns(tok, tp)[:, 0:1] - first_row
        top = jnp.max(logits, axis=1, keepdims=True)
        total = jnp.sum(jnp.exp(logits - top), axis=1, keepdims=True)
        picked = jnp.sum(jnp.where(taken, logits, 0.0), axis=1, keepdims=True)
        at = lax.broadcasted_iota(jnp.int32, (tp, LANES), 1)
        dcb[k, c] = as_rows(
            jnp.where(at == 0, top, jnp.where(at == 1, total, jnp.where(at == 2, picked, 0.0)))
        )
        a = [send(dcb.at[k, c], dcb.at[k, c], dev(c=oc))]
        yield
        arrive(a)
        dyb[k, y] = stack_rows(*combine([dcb[k, 0], dcb[k, 1]]))
        a = [send(dyb.at[k, y], dyb.at[k, y], dev(y=t)) for t in ys]
        yield
        arrive(a)
        dxb[k, x] = stack_rows(*combine([dyb[k, i] for i in range(ny)]))
        a = [send(dxb.at[k, x], dxb.at[k, x], dev(x=t)) for t in others]
        yield
        arrive(a)
        top, total, picked = combine([dxb[k, i] for i in range(NX)])
        is_own = lane[0:1] < tp
        log_norm = top + jnp.log(jnp.where(is_own, total, 1.0))
        log_prob = picked - log_norm
        ratio = jnp.minimum(jnp.exp(log_prob - tok[1:2]), tok[4:5])
        scaled = tok[3:4] * ratio * tok[2:3]
        losses.append(jnp.sum(jnp.where(is_own, scaled * log_prob, 0.0), axis=1, keepdims=True))
        cols = as_columns(stack_rows(log_norm, GRAD_SCALE * scaled, tok[0:1]), tp)
        taken = column == cols[:, 2:3] - first_row
        softmax = jnp.exp(lg[k].reshape(tp, vh) - cols[:, 0:1])
        dl = (cols[:, 1:2] * (softmax - taken.astype(F32))).astype(BF16)
        for i in range(NX):
            dlx[k, i] = dl[i * ROWS : (i + 1) * ROWS]
        for pos in range(NX):
            DL[k, c, pos, z] = dlx[k, order[pos]]
        far, near = NX - 1, pl.ds(0, NX - 1)
        a = [send(DL.at[k, c, far, z], DL.at[k, c, far, z], dev(z=t)) for t in zs]
        d = [send(DL.at[k, c, near, z], DL.at[k, c, near, z], dev(z=t)) for t in zs]
        if last:
            lossz[z] = jnp.broadcast_to(sum(losses[1:], losses[0]), (8, LANES))
            b = [send(lossz.at[z], lossz.at[z], dev(z=t)) for t in zs]
        yield
        arrive(a)
        a = [send(DL.at[k, c, far], DL.at[k, c, far], dev(c=oc))]
        yield
        arrive(a)

        def term(pos):
            d0 = DL[k, 0, pos].reshape(ny * ROWS, vh)
            d1 = DL[k, 1, pos].reshape(ny * ROWS, vh)
            t = jnp.dot(d0, w[0:vh], preferred_element_type=F32)
            t = t + jnp.dot(d1, w[vh:vl], preferred_element_type=F32)
            PB[k, pos] = t.astype(BF16).reshape(ny, ROWS, dw)

        term(3)
        a = [
            send(PB.at[k, 3, low], g1.at[k, 0], dev(x=left)),
            send(PB.at[k, 3, high], g1.at[k, 1], dev(x=right)),
        ]
        yield
        arrive(d)
        d = [send(DL.at[k, c, near], DL.at[k, c, near], dev(c=oc))]
        yield
        arrive(d)
        term(1)
        b2 = [send(PB.at[k, 1, high], g2.at[k, 0, high], dev(x=left))]
        term(2)
        b2.append(send(PB.at[k, 2, low], g2.at[k, 1, low], dev(x=right)))
        term(0)
        yield
        arrive(a)
        parts = [pl.ds(i * (dw // 2), dw // 2) for i in range(2)] if last else [pl.ds(0, dw)]
        sums = []
        for p in parts:
            gs[k, 0, :, :, p] = (PB[k, 1, low, :, p].astype(F32) + g1[k, 0, :, :, p].astype(F32)).astype(BF16)
            sums.append([send(gs.at[k, 0, :, :, p], g2.at[k, 0, low, :, p], dev(x=left))])
            gs[k, 1, :, :, p] = (PB[k, 2, high, :, p].astype(F32) + g1[k, 1, :, :, p].astype(F32)).astype(BF16)
            sums[-1].append(send(gs.at[k, 1, :, :, p], g2.at[k, 1, high, :, p], dev(x=right)))
        a = []
        for i, p in enumerate(parts):
            yield
            arrive(sums[i])
            if i == 0:
                arrive(b2)
            for t in ys + [y]:
                q = PB[k, 0, t, :, p].astype(F32)
                q = q + g2[k, 0, t, :, p].astype(F32) + g2[k, 1, t, :, p].astype(F32)
                qf[k, t, :, p] = q
                qs[k, t, :, p] = q.astype(BF16)
                if t is not y:
                    a.append(send(qs.at[k, t, :, p], qr.at[k, y, :, p], dev(y=t)))
        yield
        arrive(a)
        q = qf[k, y]
        for t in ys:
            q = q + qr[k, t].astype(F32)
        hid_ref[k * ROWS : (k + 1) * ROWS, :] = q
        if last:
            arrive(b)
            loss = lossz[0]
            for i in range(1, nz):
                loss = loss + lossz[i]
            loss_ref[0, 0] = jnp.max(loss[0:1]) * (-1.0 / (n_own * NX * ny))

    def gather():
        for k in range(1, nc):
            gather_y(k)
            yield

    def head():
        h_all = HH[...].reshape(nc * NX * ny * ROWS, dw)
        for i in range(2):
            d_all = DL[:, i].reshape(nc * NX * ny * ROWS, vh)
            t = lax.dot_general(d_all, h_all, (((0,), (0,)), ((), ())), preferred_element_type=F32)
            head_ref[i * vh : (i + 1) * vh, :] = t.astype(BF16)
        yield

    runs = {NORM: norm(), GATHER: gather(), HEAD: head()}
    runs.update((k, chunk(k)) for k in range(nc))
    for step in PLAN:
        next(runs[step], None)
    for cp in started:
        cp.wait_send()


def per_device(mesh_sizes, residual, norm_gain, head_weight, actions, behavior_logp, advantages, decision_mask, clip_tenths):
    n_grp, n_seq, n_voc = mesh_sizes
    ny, nz = n_grp * 2, n_seq // 2
    n_own, dw = residual.shape
    vl = head_weight.shape[0]
    tokens = actions.shape[0]
    nc = n_own // ROWS
    vh = vl // 2

    per_chunk = 3 * (ny - 1) + 4 * (nz - 1) + 2 + 2 + NX + 1 + (NX - 1) + 2 + 6
    n_sends = 1 + (nz - 1) + (ny - 1) + (NX - 1) + nc * per_chunk + nz - 1 + 2 + (ny - 1)
    any_space = pl.BlockSpec(memory_space=pl.ANY)
    vm = pl.BlockSpec(memory_space=pltpu.VMEM)
    tile = (8, LANES)
    loss, head_grad, hidden_grad = pl.pallas_call(
        functools.partial(kernel, ny, nz, nc),
        out_shape=(
            jax.ShapeDtypeStruct((1, 1), F32),
            jax.ShapeDtypeStruct((vl, dw), BF16),
            jax.ShapeDtypeStruct((n_own, dw), F32),
        ),
        in_specs=[any_space] * 8,
        out_specs=(pl.BlockSpec(memory_space=pltpu.SMEM), vm, vm),
        scratch_shapes=[
            pltpu.VMEM((n_own, dw), BF16),
            pltpu.VMEM((dw,), F32),
            pltpu.VMEM((vl, dw), BF16),
            pltpu.VMEM((tokens,), jnp.int32),
            pltpu.VMEM((tokens,), F32),
            pltpu.VMEM((tokens,), F32),
            pltpu.VMEM((tokens,), jnp.int32),
            pltpu.VMEM((tokens,), jnp.int32),
            pltpu.VMEM((tokens // LANES,) + tile, F32),
            pltpu.VMEM((2,) + tile, F32),
            pltpu.VMEM((nz,) + tile, F32),
            pltpu.VMEM((ny,) + tile, F32),
            pltpu.VMEM((NX,) + tile, F32),
            pltpu.VMEM((NX, LANES, LANES), F32),
            pltpu.VMEM((nc, NX, ny, ROWS, dw), BF16),
            pltpu.VMEM((nc, NX, ny, ROWS, dw), BF16),
            pltpu.VMEM((nc, NX, ny, ROWS, vh), F32),
            pltpu.VMEM((nc, NX, ny, ROWS, vh), BF16),
            pltpu.VMEM((nc, NX, ny, ROWS, vh), BF16),
            pltpu.VMEM((nc, nz, NX, ROWS, vh), BF16),
            pltpu.VMEM((nc, nz, NX, ROWS, vh), BF16),
            pltpu.VMEM((nc, NX, ROWS, vh), F32),
            pltpu.VMEM((nc, 2) + tile, F32),
            pltpu.VMEM((nc, ny) + tile, F32),
            pltpu.VMEM((nc, NX) + tile, F32),
            pltpu.VMEM((nc, NX, ROWS, vh), BF16),
            pltpu.VMEM((nc, 2, NX, ny, ROWS, vh), BF16),
            pltpu.VMEM((nc, NX, ny, ROWS, dw), BF16),
            pltpu.VMEM((nc, 2, ny // 2, ROWS, dw), BF16),
            pltpu.VMEM((nc, 2, ny, ROWS, dw), BF16),
            pltpu.VMEM((nc, 2, ny // 2, ROWS, dw), BF16),
            pltpu.VMEM((nc, ny, ROWS, dw), F32),
            pltpu.VMEM((nc, ny, ROWS, dw), BF16),
            pltpu.VMEM((nc, ny, ROWS, dw), BF16),
            pltpu.VMEM((nz,) + tile, F32),
            pltpu.SemaphoreType.DMA((8,)),
            pltpu.SemaphoreType.DMA((n_sends,)),
            pltpu.SemaphoreType.DMA((n_sends,)),
        ],
        compiler_params=pltpu.CompilerParams(
            collective_id=0, has_side_effects=True, vmem_limit_bytes=60 * 2**20
        ),
    )(residual, norm_gain, head_weight, actions, behavior_logp, advantages, decision_mask, clip_tenths)
    return loss.reshape(()), head_grad, hidden_grad


def solution(mesh):
    sizes = (mesh.shape["grp"], mesh.shape["seq"], mesh.shape["voc"])
    split = P(("grp", "voc"), "seq")
    return jax.shard_map(
        functools.partial(per_device, sizes),
        mesh=mesh,
        in_specs=(split, P("seq"), split, P(), P(), P(), P(), P()),
        out_specs=(P(), split, split),
        check_vma=False,
    )
```

```python
import functools

import jax
import jax.numpy as jnp
from jax import lax
from jax.experimental import pallas as pl
from jax.experimental.pallas import tpu as pltpu
from jax.sharding import PartitionSpec as P

EPSILON = 1e-05
GRAD_SCALE = 8.0
NX = 4
ROWS = 16
NORM, GATHER, HEAD = -1, 3, 4
PLAN = (
    -1, 3, -1, 0, -1, 3, 1, 0, -1, 0, 0, 1, 2, 0, -1, 0, 1, 1, 1, 0, 1, 2, 0, 2,
    2, 2, 0, 1, 2, 1, 0, 2, 1, 2, 0, 0, 1, 0, 2, 0, 0, 1, 2, 1, 1, 1, 1, 2,
    2, 2, 0, 2, 1, 2, 2, 2, 1, 0, 4, 2,
)
RAW = 0
FAR_FIRST = (4, 3, 5, 2, 6, 1, 7)
LANES = 128
F32 = jnp.float32
BF16 = jnp.bfloat16


def as_rows(columns):
    n = columns.shape[0]
    if n < LANES:
        columns = jnp.concatenate([columns, jnp.zeros((LANES - n, LANES), F32)], axis=0)
    return columns.T[:8]


def as_columns(rows, n):
    full = jnp.concatenate([rows, jnp.zeros((LANES - 8, LANES), F32)], axis=0)
    return full.T[:n]


def stack_rows(*rows):
    index = lax.broadcasted_iota(jnp.int32, (8, LANES), 0)
    out = jnp.zeros((8, LANES), F32)
    for i, row in enumerate(rows):
        out = jnp.where(index == i, jnp.broadcast_to(row, (8, LANES)), out)
    return out


def combine(tiles):
    top = tiles[0][0:1]
    for t in tiles[1:]:
        top = jnp.maximum(top, t[0:1])
    total = jnp.zeros_like(top)
    picked = jnp.zeros_like(top)
    for t in tiles:
        total = total + t[1:2] * jnp.exp(t[0:1] - top)
        picked = picked + t[2:3]
    return top, total, picked


def kernel(
    ny, nz, nc,
    res_hbm, gain_hbm, w_hbm, act_hbm, beh_hbm, adv_hbm, mask_hbm, clip_hbm,
    loss_ref, head_ref, hid_ref,
    res, gain, w, act, beh, adv, mask, clip, tk,
    sqc, sqz, iny, inx, invc, H, HH, Lo, xs, xr, cs, cr, lg, dcb, dyb, dxb, dlx, DL, PB,
    g1, g2, gs, qf, qs, qr, lossz, lsem, ssem, rsem,
):
    grp, seq, voc = lax.axis_index("grp"), lax.axis_index("seq"), lax.axis_index("voc")
    x, y = lax.div(voc, 2), grp * 2 + lax.rem(voc, 2)
    z, c = lax.div(seq, 2), lax.rem(seq, 2)
    oc = 1 - c
    vl, dw = w.shape
    vh = vl // 2
    tp = ROWS * NX
    n_own = res.shape[0]
    half = ny // 2
    left, right, opp = lax.rem(x + 3, NX), lax.rem(x + 1, NX), lax.rem(x + 2, NX)
    order = (x, left, right, opp)

    def dev(x=x, y=y, z=z, c=c):
        return {"grp": lax.div(y, 2), "seq": z * 2 + c, "voc": x * 2 + lax.rem(y, 2)}

    ys = [lax.rem(y + d, ny) for d in FAR_FIRST if d < ny]
    zs = [lax.rem(z + d, nz) for d in FAR_FIRST if d < nz]
    others = [opp, right, left]

    barrier = pltpu.get_barrier_semaphore()
    partners = (
        [dev(y=t) for t in ys[:3]] + [dev(z=t) for t in zs] + [dev(y=t) for t in ys[3:]]
        + [dev(x=t) for t in others] + [dev(c=oc)]
    )
    for p in partners:
        pl.semaphore_signal(barrier, inc=1, device_id=p, device_id_type=pl.DeviceIdType.MESH)

    loads = []
    pairs = ((res_hbm, res), (gain_hbm, gain), (w_hbm, w), (act_hbm, act), (beh_hbm, beh),
             (adv_hbm, adv), (mask_hbm, mask), (clip_hbm, clip))
    for i, (src, dst) in enumerate(pairs):
        loads.append(pltpu.make_async_copy(src, dst, lsem.at[i]))
        loads[-1].start()

    started = []

    def send(src, dst, target):
        i = len(started)
        cp = pltpu.make_async_remote_copy(
            src_ref=src, dst_ref=dst, send_sem=ssem.at[i], recv_sem=rsem.at[i],
            device_id=target, device_id_type=pl.DeviceIdType.MESH,
        )
        cp.start()
        started.append(cp)
        return cp

    def arrive(copies):
        for cp in copies:
            cp.wait_recv()

    loads[0].wait()
    sq = res[...].astype(F32)
    sq = sq * sq
    part = sq[:, :LANES]
    for j in range(LANES, dw, LANES):
        part = part + sq[:, j : j + LANES]
    part = jnp.concatenate([part, jnp.zeros((LANES - n_own, LANES), F32)], axis=0)
    sqc[c] = jnp.broadcast_to(jnp.sum(part.T, axis=0, keepdims=True), (8, LANES))
    for k in range(nc):
        H[k, x, y] = res[k * ROWS : (k + 1) * ROWS]
    pl.semaphore_wait(barrier, len(partners))

    gathers = {}

    def gather_y(k):
        gathers[k] = [send(H.at[k, x, y], H.at[k, x, y], dev(y=t)) for t in ys]

    def norm():
        a = [send(sqc.at[c], sqc.at[c], dev(c=oc))]
        gather_y(0)
        for cp in loads[1:]:
            cp.wait()
        n = tk.shape[0]
        vectors = [v[...].astype(F32).reshape(n, LANES) for v in (act, beh, adv, mask, clip)]
        vectors[4] = vectors[4] / 10.0
        for i in range(n):
            tk[i] = stack_rows(*[v[i : i + 1] for v in vectors])
        yield
        arrive(a)
        sqz[z] = sqc[0] + sqc[1]
        a = [send(sqz.at[z], sqz.at[z], dev(z=t)) for t in zs]
        yield
        arrive(a)
        squares = sqz[0]
        for i in range(1, nz):
            squares = squares + sqz[i]
        iny[y] = lax.rsqrt(squares / (dw * nz * 2) + EPSILON)
        a = [send(iny.at[y], iny.at[y], dev(y=t)) for t in ys]
        yield
        arrive(a)
        inx[x] = stack_rows(*[iny[i, 0:1] for i in range(ny)])
        a = [send(inx.at[x], inx.at[x], dev(x=t)) for t in others]
        yield
        arrive(a)
        rows = jnp.concatenate(
            [inx[i] for i in range(NX)] + [jnp.zeros((LANES - 8 * NX, LANES), F32)], axis=0
        )
        columns = rows.T
        for i in range(NX):
            invc[i] = pltpu.roll(columns, (LANES - 8 * i) % LANES, 1) if i else columns

    lane = lax.broadcasted_iota(jnp.int32, (8, LANES), 1)
    losses = []
    first_row = ((grp * NX * 2 + voc) * vl + c * vh).astype(F32)

    def own_tokens(k):
        out = jnp.zeros((8, LANES), F32)
        for i in range(NX):
            block = lax.div(z, 2) * (NX * 2) + i * 2 + lax.rem(z, 2)
            at = block * n_own + k * ROWS
            shift = lax.rem(LANES + i * ROWS - lax.rem(at, LANES), LANES)
            t = pltpu.roll(tk[lax.div(at, LANES)], shift, 1)
            out = jnp.where((lane >= i * ROWS) & (lane < (i + 1) * ROWS), t, out)
        return out

    def own_inv(k):
        out = jnp.zeros((1, LANES), F32)
        for i in range(NX):
            t = jnp.broadcast_to(inx[i, pl.ds(z, 1)], (8, LANES))
            shift = (LANES + (i - k) * ROWS) % LANES
            t = (pltpu.roll(t, shift, 1) if shift else t)[0:1]
            out = jnp.where((lane[0:1] >= i * ROWS) & (lane[0:1] < (i + 1) * ROWS), t, out)
        return out

    def normed(k, pos):
        at = order[pos]
        cols = invc[at]
        for j in range(ny):
            unit = H[k, at, j].astype(F32) * cols[k * ROWS : (k + 1) * ROWS, j : j + 1]
            HH[k, pos, j] = (unit * gain[...].reshape(1, dw)).astype(BF16)

    def terms(k, pos):
        at = order[pos]
        if k == RAW:
            for j in range(ny):
                HH[k, pos, j] = (H[k, at, j].astype(F32) * gain[...].reshape(1, dw)).astype(BF16)
        else:
            normed(k, pos)
        h = HH[k, pos].reshape(ny * ROWS, dw)
        w_other = w[pl.ds(pl.multiple_of(oc * vh, vh), vh)]
        t = lax.dot_general(h, w_other, (((1,), (1,)), ((), ())), preferred_element_type=F32)
        xs[k, pos] = t.astype(BF16).reshape(ny, ROWS, vh)
        cp = send(xs.at[k, pos], xr.at[k, pos], dev(c=oc))
        w_own = w[pl.ds(pl.multiple_of(c * vh, vh), vh)]
        t = lax.dot_general(h, w_own, (((1,), (1,)), ((), ())), preferred_element_type=F32)
        Lo[k, pos] = t.reshape(ny, ROWS, vh)
        return cp

    def chunk(k):
        last = k == nc - 1
        arrive(gathers[k])
        a = [send(H.at[k, x], H.at[k, x], dev(x=t)) for t in (right, left)]
        yield
        arrive(a)
        low, high = pl.ds(0, half), pl.ds(half, half)
        a = [
            send(H.at[k, left, low], H.at[k, left, low], dev(x=right)),
            send(H.at[k, right, high], H.at[k, right, high], dev(x=left)),
        ]
        yield
        b = [terms(k, pos) for pos in range(NX - 1)]
        yield
        arrive(b)
        near = pl.ds(0, NX - 1)
        b = []
        for t in zs:
            for pos in range(NX - 1):
                cs[k, t, pos] = (Lo[k, pos, t] + xr[k, pos, t].astype(F32)).astype(BF16)
            b.append(send(cs.at[k, t, near], cr.at[k, z, near], dev(z=t)))
        yield
        arrive(a)
        a = [terms(k, NX - 1)]
        yield
        arrive(a)
        far = NX - 1
        for t in zs:
            cs[k, t, far] = (Lo[k, far, t] + xr[k, far, t].astype(F32)).astype(BF16)
            b.append(send(cs.at[k, t, far], cr.at[k, z, far], dev(z=t)))
        yield
        arrive(b)
        for pos in range(NX):
            logits = Lo[k, pos, z] + xr[k, pos, z].astype(F32)
            for t in zs:
                logits = logits + cr[k, t, pos].astype(F32)
            lg[k, order[pos]] = logits
        logits = lg[k].reshape(tp, vh)
        if k == RAW:
            logits = logits * as_columns(stack_rows(own_inv(k)), tp)[:, 0:1]
            lg[k] = logits.reshape(NX, ROWS, vh)

        tok = own_tokens(k)
        column = lax.broadcasted_iota(jnp.int32, (tp, vh), 1).astype(F32)
        taken = column == as_columns(tok, tp)[:, 0:1] - first_row
        top = jnp.max(logits, axis=1, keepdims=True)
        total = jnp.sum(jnp.exp(logits - top), axis=1, keepdims=True)
        picked = jnp.sum(jnp.where(taken, logits, 0.0), axis=1, keepdims=True)
        at = lax.broadcasted_iota(jnp.int32, (tp, LANES), 1)
        dcb[k, c] = as_rows(
            jnp.where(at == 0, top, jnp.where(at == 1, total, jnp.where(at == 2, picked, 0.0)))
        )
        a = [send(dcb.at[k, c], dcb.at[k, c], dev(c=oc))]
        yield
        arrive(a)
        dyb[k, y] = stack_rows(*combine([dcb[k, 0], dcb[k, 1]]))
        a = [send(dyb.at[k, y], dyb.at[k, y], dev(y=t)) for t in ys]
        yield
        arrive(a)
        dxb[k, x] = stack_rows(*combine([dyb[k, i] for i in range(ny)]))
        a = [send(dxb.at[k, x], dxb.at[k, x], dev(x=t)) for t in others]
        yield
        arrive(a)
        top, total, picked = combine([dxb[k, i] for i in range(NX)])
        is_own = lane[0:1] < tp
        log_norm = top + jnp.log(jnp.where(is_own, total, 1.0))
        log_prob = picked - log_norm
        ratio = jnp.minimum(jnp.exp(log_prob - tok[1:2]), tok[4:5])
        scaled = tok[3:4] * ratio * tok[2:3]
        losses.append(jnp.sum(jnp.where(is_own, scaled * log_prob, 0.0), axis=1, keepdims=True))
        cols = as_columns(stack_rows(log_norm, GRAD_SCALE * scaled, tok[0:1]), tp)
        taken = column == cols[:, 2:3] - first_row
        softmax = jnp.exp(lg[k].reshape(tp, vh) - cols[:, 0:1])
        dl = (cols[:, 1:2] * (softmax - taken.astype(F32))).astype(BF16)
        for i in range(NX):
            dlx[k, i] = dl[i * ROWS : (i + 1) * ROWS]
        for pos in range(NX):
            DL[k, c, pos, z] = dlx[k, order[pos]]
        far, near = NX - 1, pl.ds(0, NX - 1)
        a = [send(DL.at[k, c, far, z], DL.at[k, c, far, z], dev(z=t)) for t in zs]
        d = [send(DL.at[k, c, near, z], DL.at[k, c, near, z], dev(z=t)) for t in zs]
        if last:
            lossz[z] = jnp.broadcast_to(sum(losses[1:], losses[0]), (8, LANES))
            b = [send(lossz.at[z], lossz.at[z], dev(z=t)) for t in zs]
        yield
        arrive(a)
        a = [send(DL.at[k, c, far], DL.at[k, c, far], dev(c=oc))]
        yield
        arrive(a)

        def term(pos):
            d0 = DL[k, 0, pos].reshape(ny * ROWS, vh)
            d1 = DL[k, 1, pos].reshape(ny * ROWS, vh)
            t = jnp.dot(d0, w[0:vh], preferred_element_type=F32)
            t = t + jnp.dot(d1, w[vh:vl], preferred_element_type=F32)
            PB[k, pos] = t.astype(BF16).reshape(ny, ROWS, dw)

        term(3)
        a = [
            send(PB.at[k, 3, low], g1.at[k, 0], dev(x=left)),
            send(PB.at[k, 3, high], g1.at[k, 1], dev(x=right)),
        ]
        yield
        arrive(d)
        d = [send(DL.at[k, c, near], DL.at[k, c, near], dev(c=oc))]
        yield
        arrive(d)
        term(1)
        b2 = [send(PB.at[k, 1, high], g2.at[k, 0, high], dev(x=left))]
        term(2)
        b2.append(send(PB.at[k, 2, low], g2.at[k, 1, low], dev(x=right)))
        term(0)
        yield
        arrive(a)
        parts = [pl.ds(i * (dw // 2), dw // 2) for i in range(2)] if last else [pl.ds(0, dw)]
        sums = []
        for p in parts:
            gs[k, 0, :, :, p] = (PB[k, 1, low, :, p].astype(F32) + g1[k, 0, :, :, p].astype(F32)).astype(BF16)
            sums.append([send(gs.at[k, 0, :, :, p], g2.at[k, 0, low, :, p], dev(x=left))])
            gs[k, 1, :, :, p] = (PB[k, 2, high, :, p].astype(F32) + g1[k, 1, :, :, p].astype(F32)).astype(BF16)
            sums[-1].append(send(gs.at[k, 1, :, :, p], g2.at[k, 1, high, :, p], dev(x=right)))
        a = []
        for i, p in enumerate(parts):
            yield
            arrive(sums[i])
            if i == 0:
                arrive(b2)
            for t in ys + [y]:
                q = PB[k, 0, t, :, p].astype(F32)
                q = q + g2[k, 0, t, :, p].astype(F32) + g2[k, 1, t, :, p].astype(F32)
                qf[k, t, :, p] = q
                qs[k, t, :, p] = q.astype(BF16)
                if t is not y:
                    a.append(send(qs.at[k, t, :, p], qr.at[k, y, :, p], dev(y=t)))
        if k == RAW:
            for pos in range(NX):
                normed(k, pos)
        yield
        arrive(a)
        q = qf[k, y]
        for t in ys:
            q = q + qr[k, t].astype(F32)
        hid_ref[k * ROWS : (k + 1) * ROWS, :] = q
        if last:
            arrive(b)
            loss = lossz[0]
            for i in range(1, nz):
                loss = loss + lossz[i]
            loss_ref[0, 0] = jnp.max(loss[0:1]) * (-1.0 / (n_own * NX * ny))

    def gather():
        for k in range(1, nc):
            gather_y(k)
            yield

    def head():
        h_all = HH[...].reshape(nc * NX * ny * ROWS, dw)
        for i in range(2):
            d_all = DL[:, i].reshape(nc * NX * ny * ROWS, vh)
            t = lax.dot_general(d_all, h_all, (((0,), (0,)), ((), ())), preferred_element_type=F32)
            head_ref[i * vh : (i + 1) * vh, :] = t.astype(BF16)
        yield

    runs = {NORM: norm(), GATHER: gather(), HEAD: head()}
    runs.update((k, chunk(k)) for k in range(nc))
    for step in PLAN:
        next(runs[step], None)
    for cp in started:
        cp.wait_send()


def per_device(mesh_sizes, residual, norm_gain, head_weight, actions, behavior_logp, advantages, decision_mask, clip_tenths):
    n_grp, n_seq, n_voc = mesh_sizes
    ny, nz = n_grp * 2, n_seq // 2
    n_own, dw = residual.shape
    vl = head_weight.shape[0]
    tokens = actions.shape[0]
    nc = n_own // ROWS
    vh = vl // 2

    per_chunk = 3 * (ny - 1) + 4 * (nz - 1) + 2 + 2 + NX + 1 + (NX - 1) + 2 + 6
    n_sends = 1 + (nz - 1) + (ny - 1) + (NX - 1) + nc * per_chunk + nz - 1 + 2 + (ny - 1)
    any_space = pl.BlockSpec(memory_space=pl.ANY)
    vm = pl.BlockSpec(memory_space=pltpu.VMEM)
    tile = (8, LANES)
    loss, head_grad, hidden_grad = pl.pallas_call(
        functools.partial(kernel, ny, nz, nc),
        out_shape=(
            jax.ShapeDtypeStruct((1, 1), F32),
            jax.ShapeDtypeStruct((vl, dw), BF16),
            jax.ShapeDtypeStruct((n_own, dw), F32),
        ),
        in_specs=[any_space] * 8,
        out_specs=(pl.BlockSpec(memory_space=pltpu.SMEM), vm, vm),
        scratch_shapes=[
            pltpu.VMEM((n_own, dw), BF16),
            pltpu.VMEM((dw,), F32),
            pltpu.VMEM((vl, dw), BF16),
            pltpu.VMEM((tokens,), jnp.int32),
            pltpu.VMEM((tokens,), F32),
            pltpu.VMEM((tokens,), F32),
            pltpu.VMEM((tokens,), jnp.int32),
            pltpu.VMEM((tokens,), jnp.int32),
            pltpu.VMEM((tokens // LANES,) + tile, F32),
            pltpu.VMEM((2,) + tile, F32),
            pltpu.VMEM((nz,) + tile, F32),
            pltpu.VMEM((ny,) + tile, F32),
            pltpu.VMEM((NX,) + tile, F32),
            pltpu.VMEM((NX, LANES, LANES), F32),
            pltpu.VMEM((nc, NX, ny, ROWS, dw), BF16),
            pltpu.VMEM((nc, NX, ny, ROWS, dw), BF16),
            pltpu.VMEM((nc, NX, ny, ROWS, vh), F32),
            pltpu.VMEM((nc, NX, ny, ROWS, vh), BF16),
            pltpu.VMEM((nc, NX, ny, ROWS, vh), BF16),
            pltpu.VMEM((nc, nz, NX, ROWS, vh), BF16),
            pltpu.VMEM((nc, nz, NX, ROWS, vh), BF16),
            pltpu.VMEM((nc, NX, ROWS, vh), F32),
            pltpu.VMEM((nc, 2) + tile, F32),
            pltpu.VMEM((nc, ny) + tile, F32),
            pltpu.VMEM((nc, NX) + tile, F32),
            pltpu.VMEM((nc, NX, ROWS, vh), BF16),
            pltpu.VMEM((nc, 2, NX, ny, ROWS, vh), BF16),
            pltpu.VMEM((nc, NX, ny, ROWS, dw), BF16),
            pltpu.VMEM((nc, 2, ny // 2, ROWS, dw), BF16),
            pltpu.VMEM((nc, 2, ny, ROWS, dw), BF16),
            pltpu.VMEM((nc, 2, ny // 2, ROWS, dw), BF16),
            pltpu.VMEM((nc, ny, ROWS, dw), F32),
            pltpu.VMEM((nc, ny, ROWS, dw), BF16),
            pltpu.VMEM((nc, ny, ROWS, dw), BF16),
            pltpu.VMEM((nz,) + tile, F32),
            pltpu.SemaphoreType.DMA((8,)),
            pltpu.SemaphoreType.DMA((n_sends,)),
            pltpu.SemaphoreType.DMA((n_sends,)),
        ],
        compiler_params=pltpu.CompilerParams(
            collective_id=0, has_side_effects=True, vmem_limit_bytes=60 * 2**20
        ),
    )(residual, norm_gain, head_weight, actions, behavior_logp, advantages, decision_mask, clip_tenths)
    return loss.reshape(()), head_grad, hidden_grad


def solution(mesh):
    sizes = (mesh.shape["grp"], mesh.shape["seq"], mesh.shape["voc"])
    split = P(("grp", "voc"), "seq")
    return jax.shard_map(
        functools.partial(per_device, sizes),
        mesh=mesh,
        in_specs=(split, P("seq"), split, P(), P(), P(), P(), P()),
        out_specs=(P(), split, split),
        check_vma=False,
    )
```

```python
import functools

import jax
import jax.numpy as jnp
from jax import lax
from jax.experimental import pallas as pl
from jax.experimental.pallas import tpu as pltpu
from jax.sharding import PartitionSpec as P

EPSILON = 1e-05
GRAD_SCALE = 8.0
NX = 4
ROWS = 16
NORM, GATHER, HEAD = -1, 3, 4
PLAN = (
    -1, -1, 0, -1, 3, 3, -1, 0, 1, -1, 0, 0, 0, 1, 2, 0, 1, 1, 1, 0, 1, 0, 2, 2,
    2, 1, 0, 1, 2, 2, 0, 1, 2, 2, 0, 1, 0, 0, 2, 0, 1, 1, 2, 0, 1, 1, 2, 1,
    2, 0, 2, 2, 1, 2, 4, 2, 0, 2, 1, 2,
)
FAR_FIRST = (4, 3, 5, 2, 6, 1, 7)
LANES = 128
F32 = jnp.float32
BF16 = jnp.bfloat16


def as_rows(columns):
    n = columns.shape[0]
    if n < LANES:
        columns = jnp.concatenate([columns, jnp.zeros((LANES - n, LANES), F32)], axis=0)
    return columns.T[:8]


def as_columns(rows, n):
    full = jnp.concatenate([rows, jnp.zeros((LANES - 8, LANES), F32)], axis=0)
    return full.T[:n]


def stack_rows(*rows):
    index = lax.broadcasted_iota(jnp.int32, (8, LANES), 0)
    out = jnp.zeros((8, LANES), F32)
    for i, row in enumerate(rows):
        out = jnp.where(index == i, jnp.broadcast_to(row, (8, LANES)), out)
    return out


def combine(tiles):
    top = tiles[0][0:1]
    for t in tiles[1:]:
        top = jnp.maximum(top, t[0:1])
    total = jnp.zeros_like(top)
    picked = jnp.zeros_like(top)
    for t in tiles:
        total = total + t[1:2] * jnp.exp(t[0:1] - top)
        picked = picked + t[2:3]
    return top, total, picked


def kernel(
    ny, nz, nc,
    res_hbm, gain_hbm, w_hbm, act_hbm, beh_hbm, adv_hbm, mask_hbm, clip_hbm,
    loss_ref, head_hbm, hid_ref,
    head_ref, res, gain, w, act, beh, adv, mask, clip, tk,
    sqc, sqz, iny, inx, invc, H, HH, Lo, xs, xr, cs, cr, lg, dcb, dyb, dxb, dlx, DL, PB,
    g1, g2, gs, qf, qs, qr, lossz, lsem, ssem, rsem,
):
    grp, seq, voc = lax.axis_index("grp"), lax.axis_index("seq"), lax.axis_index("voc")
    x, y = lax.div(voc, 2), grp * 2 + lax.rem(voc, 2)
    z, c = lax.div(seq, 2), lax.rem(seq, 2)
    oc = 1 - c
    vl, dw = w.shape
    vh = vl // 2
    tp = ROWS * NX
    n_own = res.shape[0]
    half = ny // 2
    left, right, opp = lax.rem(x + 3, NX), lax.rem(x + 1, NX), lax.rem(x + 2, NX)
    order = (x, left, right, opp)

    def dev(x=x, y=y, z=z, c=c):
        return {"grp": lax.div(y, 2), "seq": z * 2 + c, "voc": x * 2 + lax.rem(y, 2)}

    ys = [lax.rem(y + d, ny) for d in FAR_FIRST if d < ny]
    zs = [lax.rem(z + d, nz) for d in FAR_FIRST if d < nz]
    others = [opp, right, left]

    barrier = pltpu.get_barrier_semaphore()
    partners = (
        [dev(y=t) for t in ys] + [dev(z=t) for t in zs] + [dev(x=t) for t in others] + [dev(c=oc)]
    )
    for p in partners:
        pl.semaphore_signal(barrier, inc=1, device_id=p, device_id_type=pl.DeviceIdType.MESH)

    loads = []
    pairs = ((res_hbm, res), (gain_hbm, gain), (w_hbm, w), (act_hbm, act), (beh_hbm, beh),
             (adv_hbm, adv), (mask_hbm, mask), (clip_hbm, clip))
    for i, (src, dst) in enumerate(pairs):
        loads.append(pltpu.make_async_copy(src, dst, lsem.at[i]))
        loads[-1].start()

    started = []

    def send(src, dst, target):
        i = len(started)
        cp = pltpu.make_async_remote_copy(
            src_ref=src, dst_ref=dst, send_sem=ssem.at[i], recv_sem=rsem.at[i],
            device_id=target, device_id_type=pl.DeviceIdType.MESH,
        )
        cp.start()
        started.append(cp)
        return cp

    def arrive(copies):
        for cp in copies:
            cp.wait_recv()

    loads[0].wait()
    sq = res[...].astype(F32)
    sq = sq * sq
    part = sq[:, :LANES]
    for j in range(LANES, dw, LANES):
        part = part + sq[:, j : j + LANES]
    part = jnp.concatenate([part, jnp.zeros((LANES - n_own, LANES), F32)], axis=0)
    sqc[c] = jnp.broadcast_to(jnp.sum(part.T, axis=0, keepdims=True), (8, LANES))
    for k in range(nc):
        H[k, x, y] = res[k * ROWS : (k + 1) * ROWS]
    pl.semaphore_wait(barrier, len(partners))

    gathers = {}

    def gather_y(k):
        gathers[k] = [send(H.at[k, x, y], H.at[k, x, y], dev(y=t)) for t in ys]

    def norm():
        a = [send(sqc.at[c], sqc.at[c], dev(c=oc))]
        gather_y(0)
        for cp in loads[1:]:
            cp.wait()
        n = tk.shape[0]
        vectors = [v[...].astype(F32).reshape(n, LANES) for v in (act, beh, adv, mask, clip)]
        vectors[4] = vectors[4] / 10.0
        for i in range(n):
            tk[i] = stack_rows(*[v[i : i + 1] for v in vectors])
        yield
        arrive(a)
        sqz[z] = sqc[0] + sqc[1]
        a = [send(sqz.at[z], sqz.at[z], dev(z=t)) for t in zs]
        yield
        arrive(a)
        squares = sqz[0]
        for i in range(1, nz):
            squares = squares + sqz[i]
        iny[y] = lax.rsqrt(squares / (dw * nz * 2) + EPSILON)
        a = [send(iny.at[y], iny.at[y], dev(y=t)) for t in ys]
        yield
        arrive(a)
        inx[x] = stack_rows(*[iny[i, 0:1] for i in range(ny)])
        a = [send(inx.at[x], inx.at[x], dev(x=t)) for t in others]
        yield
        arrive(a)
        rows = jnp.concatenate(
            [inx[i] for i in range(NX)] + [jnp.zeros((LANES - 8 * NX, LANES), F32)], axis=0
        )
        columns = rows.T
        for i in range(NX):
            invc[i] = pltpu.roll(columns, (LANES - 8 * i) % LANES, 1) if i else columns

    lane = lax.broadcasted_iota(jnp.int32, (8, LANES), 1)
    losses = []
    first_row = ((grp * NX * 2 + voc) * vl + c * vh).astype(F32)

    def own_tokens(k):
        out = jnp.zeros((8, LANES), F32)
        for i in range(NX):
            block = lax.div(z, 2) * (NX * 2) + i * 2 + lax.rem(z, 2)
            at = block * n_own + k * ROWS
            shift = lax.rem(LANES + i * ROWS - lax.rem(at, LANES), LANES)
            t = pltpu.roll(tk[lax.div(at, LANES)], shift, 1)
            out = jnp.where((lane >= i * ROWS) & (lane < (i + 1) * ROWS), t, out)
        return out

    def terms(k, pos):
        at = order[pos]
        cols = invc[at]
        for j in range(ny):
            unit = H[k, at, j].astype(F32) * cols[k * ROWS : (k + 1) * ROWS, j : j + 1]
            HH[k, pos, j] = (unit * gain[...].reshape(1, dw)).astype(BF16)
        h = HH[k, pos].reshape(ny * ROWS, dw)
        w_other = w[pl.ds(pl.multiple_of(oc * vh, vh), vh)]
        t = lax.dot_general(h, w_other, (((1,), (1,)), ((), ())), preferred_element_type=F32)
        xs[k, pos] = t.astype(BF16).reshape(ny, ROWS, vh)
        cp = send(xs.at[k, pos], xr.at[k, pos], dev(c=oc))
        w_own = w[pl.ds(pl.multiple_of(c * vh, vh), vh)]
        t = lax.dot_general(h, w_own, (((1,), (1,)), ((), ())), preferred_element_type=F32)
        Lo[k, pos] = t.reshape(ny, ROWS, vh)
        return cp

    def chunk(k):
        last = k == nc - 1
        arrive(gathers[k])
        a = [send(H.at[k, x], H.at[k, x], dev(x=t)) for t in (right, left)]
        yield
        arrive(a)
        low, high = pl.ds(0, half), pl.ds(half, half)
        a = [
            send(H.at[k, left, low], H.at[k, left, low], dev(x=right)),
            send(H.at[k, right, high], H.at[k, right, high], dev(x=left)),
        ]
        yield
        b = [terms(k, pos) for pos in range(NX - 1)]
        yield
        arrive(b)
        near = pl.ds(0, NX - 1)
        b = []
        for t in zs:
            for pos in range(NX - 1):
                cs[k, t, pos] = (Lo[k, pos, t] + xr[k, pos, t].astype(F32)).astype(BF16)
            b.append(send(cs.at[k, t, near], cr.at[k, z, near], dev(z=t)))
        yield
        arrive(a)
        a = [terms(k, NX - 1)]
        yield
        arrive(a)
        far = NX - 1
        for t in zs:
            cs[k, t, far] = (Lo[k, far, t] + xr[k, far, t].astype(F32)).astype(BF16)
            b.append(send(cs.at[k, t, far], cr.at[k, z, far], dev(z=t)))
        yield
        arrive(b)
        for pos in range(NX):
            logits = Lo[k, pos, z] + xr[k, pos, z].astype(F32)
            for t in zs:
                logits = logits + cr[k, t, pos].astype(F32)
            lg[k, order[pos]] = logits
        logits = lg[k].reshape(tp, vh)

        tok = own_tokens(k)
        column = lax.broadcasted_iota(jnp.int32, (tp, vh), 1).astype(F32)
        taken = column == as_columns(tok, tp)[:, 0:1] - first_row
        top = jnp.max(logits, axis=1, keepdims=True)
        total = jnp.sum(jnp.exp(logits - top), axis=1, keepdims=True)
        picked = jnp.sum(jnp.where(taken, logits, 0.0), axis=1, keepdims=True)
        at = lax.broadcasted_iota(jnp.int32, (tp, LANES), 1)
        dcb[k, c] = as_rows(
            jnp.where(at == 0, top, jnp.where(at == 1, total, jnp.where(at == 2, picked, 0.0)))
        )
        a = [send(dcb.at[k, c], dcb.at[k, c], dev(c=oc))]
        yield
        arrive(a)
        dyb[k, y] = stack_rows(*combine([dcb[k, 0], dcb[k, 1]]))
        a = [send(dyb.at[k, y], dyb.at[k, y], dev(y=t)) for t in ys]
        yield
        arrive(a)
        dxb[k, x] = stack_rows(*combine([dyb[k, i] for i in range(ny)]))
        a = [send(dxb.at[k, x], dxb.at[k, x], dev(x=t)) for t in others]
        yield
        arrive(a)
        top, total, picked = combine([dxb[k, i] for i in range(NX)])
        is_own = lane[0:1] < tp
        log_norm = top + jnp.log(jnp.where(is_own, total, 1.0))
        log_prob = picked - log_norm
        ratio = jnp.minimum(jnp.exp(log_prob - tok[1:2]), tok[4:5])
        scaled = tok[3:4] * ratio * tok[2:3]
        losses.append(jnp.sum(jnp.where(is_own, scaled * log_prob, 0.0), axis=1, keepdims=True))
        cols = as_columns(stack_rows(log_norm, GRAD_SCALE * scaled, tok[0:1]), tp)
        taken = column == cols[:, 2:3] - first_row
        softmax = jnp.exp(lg[k].reshape(tp, vh) - cols[:, 0:1])
        dl = (cols[:, 1:2] * (softmax - taken.astype(F32))).astype(BF16)
        for i in range(NX):
            dlx[k, i] = dl[i * ROWS : (i + 1) * ROWS]
        for pos in range(NX):
            DL[k, c, pos, z] = dlx[k, order[pos]]
        far, near = NX - 1, pl.ds(0, NX - 1)
        a = [send(DL.at[k, c, far, z], DL.at[k, c, far, z], dev(z=t)) for t in zs]
        d = [send(DL.at[k, c, near, z], DL.at[k, c, near, z], dev(z=t)) for t in zs]
        if last:
            lossz[z] = jnp.broadcast_to(sum(losses[1:], losses[0]), (8, LANES))
            b = [send(lossz.at[z], lossz.at[z], dev(z=t)) for t in zs]
        yield
        arrive(a)
        a = [send(DL.at[k, c, far], DL.at[k, c, far], dev(c=oc))]
        yield
        arrive(a)

        def term(pos):
            d0 = DL[k, 0, pos].reshape(ny * ROWS, vh)
            d1 = DL[k, 1, pos].reshape(ny * ROWS, vh)
            t = jnp.dot(d0, w[0:vh], preferred_element_type=F32)
            t = t + jnp.dot(d1, w[vh:vl], preferred_element_type=F32)
            PB[k, pos] = t.astype(BF16).reshape(ny, ROWS, dw)

        term(3)
        a = [
            send(PB.at[k, 3, low], g1.at[k, 0], dev(x=left)),
            send(PB.at[k, 3, high], g1.at[k, 1], dev(x=right)),
        ]
        yield
        arrive(d)
        d = [send(DL.at[k, c, near], DL.at[k, c, near], dev(c=oc))]
        yield
        arrive(d)
        term(1)
        b2 = [send(PB.at[k, 1, high], g2.at[k, 0, high], dev(x=left))]
        term(2)
        b2.append(send(PB.at[k, 2, low], g2.at[k, 1, low], dev(x=right)))
        term(0)
        yield
        arrive(a)
        parts = [pl.ds(i * (dw // 2), dw // 2) for i in range(2)] if last else [pl.ds(0, dw)]
        sums = []
        for p in parts:
            gs[k, 0, :, :, p] = (PB[k, 1, low, :, p].astype(F32) + g1[k, 0, :, :, p].astype(F32)).astype(BF16)
            sums.append([send(gs.at[k, 0, :, :, p], g2.at[k, 0, low, :, p], dev(x=left))])
            gs[k, 1, :, :, p] = (PB[k, 2, high, :, p].astype(F32) + g1[k, 1, :, :, p].astype(F32)).astype(BF16)
            sums[-1].append(send(gs.at[k, 1, :, :, p], g2.at[k, 1, high, :, p], dev(x=right)))
        a = []
        for i, p in enumerate(parts):
            yield
            arrive(sums[i])
            if i == 0:
                arrive(b2)
            for t in ys + [y]:
                q = PB[k, 0, t, :, p].astype(F32)
                q = q + g2[k, 0, t, :, p].astype(F32) + g2[k, 1, t, :, p].astype(F32)
                qf[k, t, :, p] = q
                qs[k, t, :, p] = q.astype(BF16)
                if t is not y:
                    a.append(send(qs.at[k, t, :, p], qr.at[k, y, :, p], dev(y=t)))
        yield
        arrive(a)
        q = qf[k, y]
        for t in ys:
            q = q + qr[k, t].astype(F32)
        hid_ref[k * ROWS : (k + 1) * ROWS, :] = q
        if last:
            arrive(b)
            loss = lossz[0]
            for i in range(1, nz):
                loss = loss + lossz[i]
            loss_ref[0, 0] = jnp.max(loss[0:1]) * (-1.0 / (n_own * NX * ny))

    def gather():
        for k in range(1, nc):
            gather_y(k)
            yield

    stores = []

    def head():
        h_all = HH[...].reshape(nc * NX * ny * ROWS, dw)
        for i in range(2):
            d_all = DL[:, i].reshape(nc * NX * ny * ROWS, vh)
            t = lax.dot_general(d_all, h_all, (((0,), (0,)), ((), ())), preferred_element_type=F32)
            rows = pl.ds(i * vh, vh)
            head_ref[rows, :] = t.astype(BF16)
            stores.append(pltpu.make_async_copy(head_ref.at[rows], head_hbm.at[rows], lsem.at[8 + i]))
            stores[-1].start()
        yield

    runs = {NORM: norm(), GATHER: gather(), HEAD: head()}
    runs.update((k, chunk(k)) for k in range(nc))
    for step in PLAN:
        next(runs[step], None)
    for cp in started:
        cp.wait_send()
    for cp in stores:
        cp.wait()


def per_device(mesh_sizes, residual, norm_gain, head_weight, actions, behavior_logp, advantages, decision_mask, clip_tenths):
    n_grp, n_seq, n_voc = mesh_sizes
    ny, nz = n_grp * 2, n_seq // 2
    n_own, dw = residual.shape
    vl = head_weight.shape[0]
    tokens = actions.shape[0]
    nc = n_own // ROWS
    vh = vl // 2

    per_chunk = 3 * (ny - 1) + 4 * (nz - 1) + 2 + 2 + NX + 1 + (NX - 1) + 2 + 6
    n_sends = 1 + (nz - 1) + (ny - 1) + (NX - 1) + nc * per_chunk + nz - 1 + 2 + (ny - 1)
    any_space = pl.BlockSpec(memory_space=pl.ANY)
    vm = pl.BlockSpec(memory_space=pltpu.VMEM)
    tile = (8, LANES)
    loss, head_grad, hidden_grad = pl.pallas_call(
        functools.partial(kernel, ny, nz, nc),
        out_shape=(
            jax.ShapeDtypeStruct((1, 1), F32),
            jax.ShapeDtypeStruct((vl, dw), BF16),
            jax.ShapeDtypeStruct((n_own, dw), F32),
        ),
        in_specs=[any_space] * 8,
        out_specs=(pl.BlockSpec(memory_space=pltpu.SMEM), any_space, vm),
        scratch_shapes=[
            pltpu.VMEM((vl, dw), BF16),
            pltpu.VMEM((n_own, dw), BF16),
            pltpu.VMEM((dw,), F32),
            pltpu.VMEM((vl, dw), BF16),
            pltpu.VMEM((tokens,), jnp.int32),
            pltpu.VMEM((tokens,), F32),
            pltpu.VMEM((tokens,), F32),
            pltpu.VMEM((tokens,), jnp.int32),
            pltpu.VMEM((tokens,), jnp.int32),
            pltpu.VMEM((tokens // LANES,) + tile, F32),
            pltpu.VMEM((2,) + tile, F32),
            pltpu.VMEM((nz,) + tile, F32),
            pltpu.VMEM((ny,) + tile, F32),
            pltpu.VMEM((NX,) + tile, F32),
            pltpu.VMEM((NX, LANES, LANES), F32),
            pltpu.VMEM((nc, NX, ny, ROWS, dw), BF16),
            pltpu.VMEM((nc, NX, ny, ROWS, dw), BF16),
            pltpu.VMEM((nc, NX, ny, ROWS, vh), F32),
            pltpu.VMEM((nc, NX, ny, ROWS, vh), BF16),
            pltpu.VMEM((nc, NX, ny, ROWS, vh), BF16),
            pltpu.VMEM((nc, nz, NX, ROWS, vh), BF16),
            pltpu.VMEM((nc, nz, NX, ROWS, vh), BF16),
            pltpu.VMEM((nc, NX, ROWS, vh), F32),
            pltpu.VMEM((nc, 2) + tile, F32),
            pltpu.VMEM((nc, ny) + tile, F32),
            pltpu.VMEM((nc, NX) + tile, F32),
            pltpu.VMEM((nc, NX, ROWS, vh), BF16),
            pltpu.VMEM((nc, 2, NX, ny, ROWS, vh), BF16),
            pltpu.VMEM((nc, NX, ny, ROWS, dw), BF16),
            pltpu.VMEM((nc, 2, ny // 2, ROWS, dw), BF16),
            pltpu.VMEM((nc, 2, ny, ROWS, dw), BF16),
            pltpu.VMEM((nc, 2, ny // 2, ROWS, dw), BF16),
            pltpu.VMEM((nc, ny, ROWS, dw), F32),
            pltpu.VMEM((nc, ny, ROWS, dw), BF16),
            pltpu.VMEM((nc, ny, ROWS, dw), BF16),
            pltpu.VMEM((nz,) + tile, F32),
            pltpu.SemaphoreType.DMA((10,)),
            pltpu.SemaphoreType.DMA((n_sends,)),
            pltpu.SemaphoreType.DMA((n_sends,)),
        ],
        compiler_params=pltpu.CompilerParams(
            collective_id=0, has_side_effects=True, vmem_limit_bytes=60 * 2**20
        ),
    )(residual, norm_gain, head_weight, actions, behavior_logp, advantages, decision_mask, clip_tenths)
    return loss.reshape(()), head_grad, hidden_grad


def solution(mesh):
    sizes = (mesh.shape["grp"], mesh.shape["seq"], mesh.shape["voc"])
    split = P(("grp", "voc"), "seq")
    return jax.shard_map(
        functools.partial(per_device, sizes),
        mesh=mesh,
        in_specs=(split, P("seq"), split, P(), P(), P(), P(), P()),
        out_specs=(P(), split, split),
        check_vma=False,
    )
```

```python
import functools

import jax
import jax.numpy as jnp
from jax import lax
from jax.experimental import pallas as pl
from jax.experimental.pallas import tpu as pltpu
from jax.sharding import PartitionSpec as P

EPSILON = 1e-05
GRAD_SCALE = 8.0
NX = 4
ROWS = 16
NORM, GATHER, HEAD = -1, 3, 4
PLAN = (
    -1, -1, 0, -1, 3, 3, -1, 0, 1, -1, 0, 0, 0, 1, 2, 0, 1, 1, 1, 0, 1, 0, 2, 2,
    2, 1, 0, 1, 2, 2, 0, 1, 2, 2, 0, 1, 0, 0, 2, 0, 1, 1, 2, 0, 1, 1, 2, 1,
    2, 0, 2, 2, 1, 2, 4, 2, 0, 2, 1, 2,
)
FAR_FIRST = (4, 3, 5, 2, 6, 1, 7)
LANES = 128
F32 = jnp.float32
BF16 = jnp.bfloat16


def as_rows(columns):
    n = columns.shape[0]
    if n < LANES:
        columns = jnp.concatenate([columns, jnp.zeros((LANES - n, LANES), F32)], axis=0)
    return columns.T[:8]


def as_columns(rows, n):
    full = jnp.concatenate([rows, jnp.zeros((LANES - 8, LANES), F32)], axis=0)
    return full.T[:n]


def stack_rows(*rows):
    index = lax.broadcasted_iota(jnp.int32, (8, LANES), 0)
    out = jnp.zeros((8, LANES), F32)
    for i, row in enumerate(rows):
        out = jnp.where(index == i, jnp.broadcast_to(row, (8, LANES)), out)
    return out


def combine(tiles):
    top = tiles[0][0:1]
    for t in tiles[1:]:
        top = jnp.maximum(top, t[0:1])
    total = jnp.zeros_like(top)
    picked = jnp.zeros_like(top)
    for t in tiles:
        total = total + t[1:2] * jnp.exp(t[0:1] - top)
        picked = picked + t[2:3]
    return top, total, picked


def kernel(
    ny, nz, nc,
    res_hbm, gain_hbm, w_hbm, act_hbm, beh_hbm, adv_hbm, mask_hbm, clip_hbm,
    loss_ref, head_hbm, hid_ref,
    head_ref, res, gain, w, act, beh, adv, mask, clip, tk,
    sqc, sqz, iny, inx, invc, H, HH, Lo, xs, xr, cs, cr, lg, dcb, dyb, dxb, dlx, DL, PB,
    g1, g2, gs, qf, qs, qr, lossz, lsem, ssem, rsem,
):
    grp, seq, voc = lax.axis_index("grp"), lax.axis_index("seq"), lax.axis_index("voc")
    x, y = lax.div(voc, 2), grp * 2 + lax.rem(voc, 2)
    z, c = lax.div(seq, 2), lax.rem(seq, 2)
    oc = 1 - c
    vl, dw = w.shape
    vh = vl // 2
    tp = ROWS * NX
    n_own = res.shape[0]
    half = ny // 2
    left, right, opp = lax.rem(x + 3, NX), lax.rem(x + 1, NX), lax.rem(x + 2, NX)
    order = (x, left, right, opp)

    def dev(x=x, y=y, z=z, c=c):
        return {"grp": lax.div(y, 2), "seq": z * 2 + c, "voc": x * 2 + lax.rem(y, 2)}

    ys = [lax.rem(y + d, ny) for d in FAR_FIRST if d < ny]
    zs = [lax.rem(z + d, nz) for d in FAR_FIRST if d < nz]
    others = [opp, right, left]

    barrier = pltpu.get_barrier_semaphore()
    partners = (
        [dev(y=t) for t in ys] + [dev(z=t) for t in zs] + [dev(x=t) for t in others] + [dev(c=oc)]
    )
    for p in partners:
        pl.semaphore_signal(barrier, inc=1, device_id=p, device_id_type=pl.DeviceIdType.MESH)

    loads = []
    pairs = ((res_hbm, res), (gain_hbm, gain), (w_hbm, w), (act_hbm, act), (beh_hbm, beh),
             (adv_hbm, adv), (mask_hbm, mask), (clip_hbm, clip))
    for i, (src, dst) in enumerate(pairs):
        loads.append(pltpu.make_async_copy(src, dst, lsem.at[i]))
        loads[-1].start()

    started = []

    def send(src, dst, target):
        i = len(started)
        cp = pltpu.make_async_remote_copy(
            src_ref=src, dst_ref=dst, send_sem=ssem.at[i], recv_sem=rsem.at[i],
            device_id=target, device_id_type=pl.DeviceIdType.MESH,
        )
        cp.start()
        started.append(cp)
        return cp

    def arrive(copies):
        for cp in copies:
            cp.wait_recv()

    loads[0].wait()
    sq = res[...].astype(F32)
    sq = sq * sq
    part = sq[:, :LANES]
    for j in range(LANES, dw, LANES):
        part = part + sq[:, j : j + LANES]
    part = jnp.concatenate([part, jnp.zeros((LANES - n_own, LANES), F32)], axis=0)
    sqc[c] = jnp.broadcast_to(jnp.sum(part.T, axis=0, keepdims=True), (8, LANES))
    for k in range(nc):
        H[k, x, y] = res[k * ROWS : (k + 1) * ROWS]
    pl.semaphore_wait(barrier, len(partners))

    gathers = {}

    def gather_y(k):
        gathers[k] = [send(H.at[k, x, y], H.at[k, x, y], dev(y=t)) for t in ys]

    def norm():
        a = [send(sqc.at[c], sqc.at[c], dev(c=oc))]
        gather_y(0)
        for cp in loads[1:]:
            cp.wait()
        n = tk.shape[0]
        vectors = [v[...].astype(F32).reshape(n, LANES) for v in (act, beh, adv, mask, clip)]
        vectors[4] = vectors[4] / 10.0
        for i in range(n):
            tk[i] = stack_rows(*[v[i : i + 1] for v in vectors])
        yield
        arrive(a)
        sqz[z] = sqc[0] + sqc[1]
        a = [send(sqz.at[z], sqz.at[z], dev(z=t)) for t in zs]
        yield
        arrive(a)
        squares = sqz[0]
        for i in range(1, nz):
            squares = squares + sqz[i]
        iny[y] = lax.rsqrt(squares / (dw * nz * 2) + EPSILON)
        a = [send(iny.at[y], iny.at[y], dev(y=t)) for t in ys]
        yield
        arrive(a)
        inx[x] = stack_rows(*[iny[i, 0:1] for i in range(ny)])
        a = [send(inx.at[x], inx.at[x], dev(x=t)) for t in others]
        yield
        arrive(a)
        rows = jnp.concatenate(
            [inx[i] for i in range(NX)] + [jnp.zeros((LANES - 8 * NX, LANES), F32)], axis=0
        )
        columns = rows.T
        for i in range(NX):
            invc[i] = pltpu.roll(columns, (LANES - 8 * i) % LANES, 1) if i else columns

    lane = lax.broadcasted_iota(jnp.int32, (8, LANES), 1)
    losses = []
    first_row = ((grp * NX * 2 + voc) * vl + c * vh).astype(F32)

    def own_tokens(k):
        out = jnp.zeros((8, LANES), F32)
        for i in range(NX):
            block = lax.div(z, 2) * (NX * 2) + i * 2 + lax.rem(z, 2)
            at = block * n_own + k * ROWS
            shift = lax.rem(LANES + i * ROWS - lax.rem(at, LANES), LANES)
            t = pltpu.roll(tk[lax.div(at, LANES)], shift, 1)
            out = jnp.where((lane >= i * ROWS) & (lane < (i + 1) * ROWS), t, out)
        return out

    def terms(k, pos):
        at = order[pos]
        cols = invc[at]
        for j in range(ny):
            unit = H[k, at, j].astype(F32) * cols[k * ROWS : (k + 1) * ROWS, j : j + 1]
            HH[k, pos, j] = (unit * gain[...].reshape(1, dw)).astype(BF16)
        h = HH[k, pos].reshape(ny * ROWS, dw)
        w_other = w[pl.ds(pl.multiple_of(oc * vh, vh), vh)]
        t = lax.dot_general(h, w_other, (((1,), (1,)), ((), ())), preferred_element_type=F32)
        xs[k, pos] = t.astype(BF16).reshape(ny, ROWS, vh)
        cp = send(xs.at[k, pos], xr.at[k, pos], dev(c=oc))
        w_own = w[pl.ds(pl.multiple_of(c * vh, vh), vh)]
        t = lax.dot_general(h, w_own, (((1,), (1,)), ((), ())), preferred_element_type=F32)
        Lo[k, pos] = t.reshape(ny, ROWS, vh)
        return cp

    def chunk(k):
        last = k == nc - 1
        arrive(gathers[k])
        low, high = pl.ds(0, half), pl.ds(half, half)
        a = [send(H.at[k, x, p], H.at[k, x, p], dev(x=t)) for t, p in ((right, low), (left, high))]
        b = [send(H.at[k, x, p], H.at[k, x, p], dev(x=t)) for t, p in ((right, high), (left, low))]
        yield
        arrive(a)
        a = [
            send(H.at[k, left, low], H.at[k, left, low], dev(x=right)),
            send(H.at[k, right, high], H.at[k, right, high], dev(x=left)),
        ]
        yield
        arrive(b)
        b = [terms(k, pos) for pos in range(NX - 1)]
        yield
        arrive(b)
        near = pl.ds(0, NX - 1)
        b = []
        for t in zs:
            for pos in range(NX - 1):
                cs[k, t, pos] = (Lo[k, pos, t] + xr[k, pos, t].astype(F32)).astype(BF16)
            b.append(send(cs.at[k, t, near], cr.at[k, z, near], dev(z=t)))
        yield
        arrive(a)
        a = [terms(k, NX - 1)]
        yield
        arrive(a)
        far = NX - 1
        for t in zs:
            cs[k, t, far] = (Lo[k, far, t] + xr[k, far, t].astype(F32)).astype(BF16)
            b.append(send(cs.at[k, t, far], cr.at[k, z, far], dev(z=t)))
        yield
        arrive(b)
        for pos in range(NX):
            logits = Lo[k, pos, z] + xr[k, pos, z].astype(F32)
            for t in zs:
                logits = logits + cr[k, t, pos].astype(F32)
            lg[k, order[pos]] = logits
        logits = lg[k].reshape(tp, vh)

        tok = own_tokens(k)
        column = lax.broadcasted_iota(jnp.int32, (tp, vh), 1).astype(F32)
        taken = column == as_columns(tok, tp)[:, 0:1] - first_row
        top = jnp.max(logits, axis=1, keepdims=True)
        total = jnp.sum(jnp.exp(logits - top), axis=1, keepdims=True)
        picked = jnp.sum(jnp.where(taken, logits, 0.0), axis=1, keepdims=True)
        at = lax.broadcasted_iota(jnp.int32, (tp, LANES), 1)
        dcb[k, c] = as_rows(
            jnp.where(at == 0, top, jnp.where(at == 1, total, jnp.where(at == 2, picked, 0.0)))
        )
        a = [send(dcb.at[k, c], dcb.at[k, c], dev(c=oc))]
        yield
        arrive(a)
        dyb[k, y] = stack_rows(*combine([dcb[k, 0], dcb[k, 1]]))
        a = [send(dyb.at[k, y], dyb.at[k, y], dev(y=t)) for t in ys]
        yield
        arrive(a)
        dxb[k, x] = stack_rows(*combine([dyb[k, i] for i in range(ny)]))
        a = [send(dxb.at[k, x], dxb.at[k, x], dev(x=t)) for t in others]
        yield
        arrive(a)
        top, total, picked = combine([dxb[k, i] for i in range(NX)])
        is_own = lane[0:1] < tp
        log_norm = top + jnp.log(jnp.where(is_own, total, 1.0))
        log_prob = picked - log_norm
        ratio = jnp.minimum(jnp.exp(log_prob - tok[1:2]), tok[4:5])
        scaled = tok[3:4] * ratio * tok[2:3]
        losses.append(jnp.sum(jnp.where(is_own, scaled * log_prob, 0.0), axis=1, keepdims=True))
        cols = as_columns(stack_rows(log_norm, GRAD_SCALE * scaled, tok[0:1]), tp)
        taken = column == cols[:, 2:3] - first_row
        softmax = jnp.exp(lg[k].reshape(tp, vh) - cols[:, 0:1])
        dl = (cols[:, 1:2] * (softmax - taken.astype(F32))).astype(BF16)
        for i in range(NX):
            dlx[k, i] = dl[i * ROWS : (i + 1) * ROWS]
        for pos in range(NX):
            DL[k, c, pos, z] = dlx[k, order[pos]]
        far, near = NX - 1, pl.ds(0, NX - 1)
        a = [send(DL.at[k, c, far, z], DL.at[k, c, far, z], dev(z=t)) for t in zs]
        d = [send(DL.at[k, c, near, z], DL.at[k, c, near, z], dev(z=t)) for t in zs]
        if last:
            lossz[z] = jnp.broadcast_to(sum(losses[1:], losses[0]), (8, LANES))
            b = [send(lossz.at[z], lossz.at[z], dev(z=t)) for t in zs]
        yield
        arrive(a)
        a = [send(DL.at[k, c, far], DL.at[k, c, far], dev(c=oc))]
        yield
        arrive(a)

        def term(pos):
            d0 = DL[k, 0, pos].reshape(ny * ROWS, vh)
            d1 = DL[k, 1, pos].reshape(ny * ROWS, vh)
            t = jnp.dot(d0, w[0:vh], preferred_element_type=F32)
            t = t + jnp.dot(d1, w[vh:vl], preferred_element_type=F32)
            PB[k, pos] = t.astype(BF16).reshape(ny, ROWS, dw)

        term(3)
        a = [
            send(PB.at[k, 3, low], g1.at[k, 0], dev(x=left)),
            send(PB.at[k, 3, high], g1.at[k, 1], dev(x=right)),
        ]
        yield
        arrive(d)
        d = [send(DL.at[k, c, near], DL.at[k, c, near], dev(c=oc))]
        yield
        arrive(d)
        term(1)
        b2 = [send(PB.at[k, 1, high], g2.at[k, 0, high], dev(x=left))]
        term(2)
        b2.append(send(PB.at[k, 2, low], g2.at[k, 1, low], dev(x=right)))
        term(0)
        yield
        arrive(a)
        parts = [pl.ds(i * (dw // 2), dw // 2) for i in range(2)] if last else [pl.ds(0, dw)]
        sums = []
        for p in parts:
            gs[k, 0, :, :, p] = (PB[k, 1, low, :, p].astype(F32) + g1[k, 0, :, :, p].astype(F32)).astype(BF16)
            sums.append([send(gs.at[k, 0, :, :, p], g2.at[k, 0, low, :, p], dev(x=left))])
            gs[k, 1, :, :, p] = (PB[k, 2, high, :, p].astype(F32) + g1[k, 1, :, :, p].astype(F32)).astype(BF16)
            sums[-1].append(send(gs.at[k, 1, :, :, p], g2.at[k, 1, high, :, p], dev(x=right)))
        a = []
        for i, p in enumerate(parts):
            yield
            arrive(sums[i])
            if i == 0:
                arrive(b2)
            for t in ys + [y]:
                q = PB[k, 0, t, :, p].astype(F32)
                q = q + g2[k, 0, t, :, p].astype(F32) + g2[k, 1, t, :, p].astype(F32)
                qf[k, t, :, p] = q
                qs[k, t, :, p] = q.astype(BF16)
                if t is not y:
                    a.append(send(qs.at[k, t, :, p], qr.at[k, y, :, p], dev(y=t)))
        yield
        arrive(a)
        q = qf[k, y]
        for t in ys:
            q = q + qr[k, t].astype(F32)
        hid_ref[k * ROWS : (k + 1) * ROWS, :] = q
        if last:
            arrive(b)
            loss = lossz[0]
            for i in range(1, nz):
                loss = loss + lossz[i]
            loss_ref[0, 0] = jnp.max(loss[0:1]) * (-1.0 / (n_own * NX * ny))

    def gather():
        for k in range(1, nc):
            gather_y(k)
            yield

    stores = []

    def head():
        h_all = HH[...].reshape(nc * NX * ny * ROWS, dw)
        for i in range(2):
            d_all = DL[:, i].reshape(nc * NX * ny * ROWS, vh)
            t = lax.dot_general(d_all, h_all, (((0,), (0,)), ((), ())), preferred_element_type=F32)
            rows = pl.ds(i * vh, vh)
            head_ref[rows, :] = t.astype(BF16)
            stores.append(pltpu.make_async_copy(head_ref.at[rows], head_hbm.at[rows], lsem.at[8 + i]))
            stores[-1].start()
        yield

    runs = {NORM: norm(), GATHER: gather(), HEAD: head()}
    runs.update((k, chunk(k)) for k in range(nc))
    for step in PLAN:
        next(runs[step], None)
    for cp in started:
        cp.wait_send()
    for cp in stores:
        cp.wait()


def per_device(mesh_sizes, residual, norm_gain, head_weight, actions, behavior_logp, advantages, decision_mask, clip_tenths):
    n_grp, n_seq, n_voc = mesh_sizes
    ny, nz = n_grp * 2, n_seq // 2
    n_own, dw = residual.shape
    vl = head_weight.shape[0]
    tokens = actions.shape[0]
    nc = n_own // ROWS
    vh = vl // 2

    per_chunk = 3 * (ny - 1) + 4 * (nz - 1) + 4 + 2 + NX + 1 + (NX - 1) + 2 + 6
    n_sends = 1 + (nz - 1) + (ny - 1) + (NX - 1) + nc * per_chunk + nz - 1 + 2 + (ny - 1)
    any_space = pl.BlockSpec(memory_space=pl.ANY)
    vm = pl.BlockSpec(memory_space=pltpu.VMEM)
    tile = (8, LANES)
    loss, head_grad, hidden_grad = pl.pallas_call(
        functools.partial(kernel, ny, nz, nc),
        out_shape=(
            jax.ShapeDtypeStruct((1, 1), F32),
            jax.ShapeDtypeStruct((vl, dw), BF16),
            jax.ShapeDtypeStruct((n_own, dw), F32),
        ),
        in_specs=[any_space] * 8,
        out_specs=(pl.BlockSpec(memory_space=pltpu.SMEM), any_space, vm),
        scratch_shapes=[
            pltpu.VMEM((vl, dw), BF16),
            pltpu.VMEM((n_own, dw), BF16),
            pltpu.VMEM((dw,), F32),
            pltpu.VMEM((vl, dw), BF16),
            pltpu.VMEM((tokens,), jnp.int32),
            pltpu.VMEM((tokens,), F32),
            pltpu.VMEM((tokens,), F32),
            pltpu.VMEM((tokens,), jnp.int32),
            pltpu.VMEM((tokens,), jnp.int32),
            pltpu.VMEM((tokens // LANES,) + tile, F32),
            pltpu.VMEM((2,) + tile, F32),
            pltpu.VMEM((nz,) + tile, F32),
            pltpu.VMEM((ny,) + tile, F32),
            pltpu.VMEM((NX,) + tile, F32),
            pltpu.VMEM((NX, LANES, LANES), F32),
            pltpu.VMEM((nc, NX, ny, ROWS, dw), BF16),
            pltpu.VMEM((nc, NX, ny, ROWS, dw), BF16),
            pltpu.VMEM((nc, NX, ny, ROWS, vh), F32),
            pltpu.VMEM((nc, NX, ny, ROWS, vh), BF16),
            pltpu.VMEM((nc, NX, ny, ROWS, vh), BF16),
            pltpu.VMEM((nc, nz, NX, ROWS, vh), BF16),
            pltpu.VMEM((nc, nz, NX, ROWS, vh), BF16),
            pltpu.VMEM((nc, NX, ROWS, vh), F32),
            pltpu.VMEM((nc, 2) + tile, F32),
            pltpu.VMEM((nc, ny) + tile, F32),
            pltpu.VMEM((nc, NX) + tile, F32),
            pltpu.VMEM((nc, NX, ROWS, vh), BF16),
            pltpu.VMEM((nc, 2, NX, ny, ROWS, vh), BF16),
            pltpu.VMEM((nc, NX, ny, ROWS, dw), BF16),
            pltpu.VMEM((nc, 2, ny // 2, ROWS, dw), BF16),
            pltpu.VMEM((nc, 2, ny, ROWS, dw), BF16),
            pltpu.VMEM((nc, 2, ny // 2, ROWS, dw), BF16),
            pltpu.VMEM((nc, ny, ROWS, dw), F32),
            pltpu.VMEM((nc, ny, ROWS, dw), BF16),
            pltpu.VMEM((nc, ny, ROWS, dw), BF16),
            pltpu.VMEM((nz,) + tile, F32),
            pltpu.SemaphoreType.DMA((10,)),
            pltpu.SemaphoreType.DMA((n_sends,)),
            pltpu.SemaphoreType.DMA((n_sends,)),
        ],
        compiler_params=pltpu.CompilerParams(
            collective_id=0, has_side_effects=True, vmem_limit_bytes=60 * 2**20
        ),
    )(residual, norm_gain, head_weight, actions, behavior_logp, advantages, decision_mask, clip_tenths)
    return loss.reshape(()), head_grad, hidden_grad


def solution(mesh):
    sizes = (mesh.shape["grp"], mesh.shape["seq"], mesh.shape["voc"])
    split = P(("grp", "voc"), "seq")
    return jax.shard_map(
        functools.partial(per_device, sizes),
        mesh=mesh,
        in_specs=(split, P("seq"), split, P(), P(), P(), P(), P()),
        out_specs=(P(), split, split),
        check_vma=False,
    )
```
